128 devices in a mesh: grp: 2 (over x_lo), px: 8 (over y, core), pz: 8 (over x_hi, z).
Axes of the slice: x: 4 (x_hi: 2, x_lo: 2; x = x_hi * 2 + x_lo), y: 4, z: 4, core: 2. Of those that a mesh axis runs over, the one named last changes fastest.
Arguments:
- cell_index: int32 [4096, 512], P(('px', 'pz')), may hold values from 0 to 255
- block_index: int32 [4096], P(('px', 'pz')), may hold values from 0 to 63
- volume: float32 [4096, 512], P(('px', 'pz')), may hold values from 0.2 to 2
- response_rate: float32 [4096, 512], P(('px', 'pz')), may hold values from 0.2 to 2
- spanwise_position: float32 [4096, 512], P(('px', 'pz')), may hold values from -3.140625 to 3.140625
- particle_velocity: float32 [3, 4096, 512], P(None, ('px', 'pz')), may hold values from -6 to 6
- seen_velocity: float32 [3, 4096, 512], P(None, ('px', 'pz')), may hold values from -6 to 6
- fluid_velocity: float32 [512, 3, 16, 2, 1024], P(None, None, ('grp', 'pz'), None, 'px'), may hold values from -6 to 6
- eigen_basis: float32 [512, 512], replicated, may hold values from -1 to 2, as said below
- eigen_inverse: float32 [512, 512], replicated, may hold values from -8 to 8, as said below
- eigenvalues: float32 [512], replicated, may hold values from 1 to 100000
Outputs:
- velocity_planes: bfloat16 [512, 3, 16, 2, 2048], P(('px', 'pz'), None, 'grp')
- updated_velocity: float32 [3, 4096, 512], P(None, ('px', 'pz'))
The draws below stay inside these ranges and needn't reach their ends.
Inputs may be any that keep to these rules, and one draw needn't show every extreme that they name: eigen_inverse is the inverse of eigen_basis. eigen_basis has a dominant unit diagonal.
All inputs are finite; a program needn't handle non-finite values.
Results may differ from the reference program's by a relative error of at most 0.007.
Values may be sent and summed in bfloat16 or wider, within the bound.
A program may use at most 128 MiB of HBM per device.

```python
import math
import jax
import jax.numpy as jnp
from jax import lax

NX = 2048
KX = 1024
NY = 512
CB = 256
PT = 512
TILE_DEV = 64
MZ = 16
NB = 64
TILES = 4096
N_PX = 8
N_PZ = 8


def basis_matrix(key):
    sub_key = jax.random.fold_in(key, 17)
    noise = jax.random.normal(sub_key, (NY, NY), jnp.float32)
    return jnp.eye(NY, dtype=jnp.float32) + 0.5 * noise / math.sqrt(NY)


def draw_eigen_basis(key, part):
    return basis_matrix(key)


def draw_eigen_inverse(key, part):
    return jnp.linalg.inv(basis_matrix(key))


def plant(values, key, low, high):
    index_at = [jax.random.randint(jax.random.fold_in(key, axis), (), 0, length) for axis, length in enumerate(values.shape)]
    widest = values.shape.index(max(values.shape))
    neighbour = index_at[:widest] + [(index_at[widest] + 1) % values.shape[widest]] + index_at[widest + 1:]
    return values.at[tuple(index_at)].set(low).at[tuple(neighbour)].set(high)


def block_scale(rng, extent, cuts, least, top_value):
    gain, own = 1.0, jax.random.fold_in(rng, 6)
    for dim, parts in cuts:
        steps = jnp.exp(jax.random.uniform(jax.random.fold_in(own, dim), (parts,), jnp.float32, least / len(cuts), top_value / len(cuts)))
        gain = gain * jnp.repeat(steps, extent[dim] // parts).reshape([-1 if axis == dim else 1 for axis in range(len(extent))])
    return gain


def normal_values(own_key, dims, spread, most, cuts=(), kind=jnp.bfloat16):
    entries = spread * jax.random.normal(own_key, dims, jnp.float32)
    if cuts:
        entries = entries * block_scale(own_key, dims, cuts, -0.22, 0.18)
    return jnp.clip(entries, -most, most).astype(kind)


def setup_inputs(seed: int = 0) -> dict:
    seeds = jax.random.split(jax.random.key(seed), 12)
    cell_index = plant(jax.random.randint(seeds[0], (TILES, PT), 0, CB), jax.random.fold_in(seeds[0], 1), 0, CB - 1).astype(jnp.int32)
    block_index = plant(jax.random.randint(seeds[1], (TILES,), 0, NB), jax.random.fold_in(seeds[1], 1), 0, NB - 1).astype(jnp.int32)
    volume = jnp.clip(jnp.exp(math.log(2.0) - 2.3025851 * jax.random.uniform(seeds[2], (TILES, PT), jnp.float32) ** block_scale(seeds[2], (TILES, PT), ((0, 64),), -0.2, 0.2)), 0.2, 2.0)
    response_rate = jnp.clip(jnp.exp(math.log(2.0) - 2.3025851 * jax.random.uniform(seeds[3], (TILES, PT), jnp.float32) ** block_scale(seeds[3], (TILES, PT), ((0, 64),), -0.2, 0.2)), 0.2, 2.0)
    spanwise_position = jnp.clip(jax.random.uniform(seeds[4], (TILES, PT), jnp.float32, -3.140625, 3.140625), -3.140625, 3.140625)
    particle_velocity = normal_values(seeds[5], (3, TILES, PT), 1.0, 6.0, ((1, 64),), jnp.float32)
    seen_velocity = normal_values(seeds[6], (3, TILES, PT), 1.0, 6.0, ((1, 64),), jnp.float32)
    fluid_velocity = normal_values(seeds[7], (NY, 3, MZ, 2, KX), 1.0, 6.0, ((2, 16), (4, 8)), jnp.float32)
    eigen_basis = draw_eigen_basis(jax.random.fold_in(seeds[11], 71), 0)
    eigen_inverse = draw_eigen_inverse(jax.random.fold_in(seeds[11], 71), 0)
    eigenvalues = jnp.clip(jnp.exp(jax.random.uniform(seeds[10], (NY,), jnp.float32, math.log(1.0), math.log(100000.0))), 1.0, 100000.0)
    return dict(cell_index=cell_index, block_index=block_index, volume=volume, response_rate=response_rate, spanwise_position=spanwise_position, particle_velocity=particle_velocity, seen_velocity=seen_velocity, fluid_velocity=fluid_velocity, eigen_basis=eigen_basis, eigen_inverse=eigen_inverse, eigenvalues=eigenvalues)


time_step = 0.5
gravity = 0.8
viscosity = 0.0001

def wave_table():
    positions = jnp.arange(NX, dtype=jnp.int32)
    stream_waves = jnp.arange(KX, dtype=jnp.int32) - KX // 2
    phase_turns = jnp.mod(positions[:, None] * stream_waves[None, :], NX)
    angles = phase_turns.astype(jnp.float32) * (2.0 * math.pi / NX)
    factor = 1.0 / math.sqrt(NX)
    return jnp.stack([jnp.cos(angles) * factor, jnp.sin(angles) * factor], axis=1).astype(jnp.bfloat16)

def reference(cell_index, block_index, volume, response_rate, spanwise_position, particle_velocity, seen_velocity, fluid_velocity, eigen_basis, eigen_inverse, eigenvalues):
    slabs = N_PX * N_PZ
    slab_rows = NY // slabs
    strips = NX // CB
    highest = lax.Precision.HIGHEST
    forward_waves = wave_table()
    forward_float = forward_waves.astype(jnp.float32).reshape(strips, CB, 2, KX)
    inverse_float = jnp.transpose(forward_waves, (2, 1, 0)).astype(jnp.float32)
    spanwise_waves = (jnp.arange(MZ) + 1).astype(jnp.float32)
    lanes = jnp.arange(CB, dtype=jnp.int32)
    cell_slabs = cell_index.reshape(slabs, TILE_DEV, PT)
    block_slabs = block_index.reshape(slabs, TILE_DEV)
    volume_slabs = volume.reshape(slabs, TILE_DEV, PT)
    rate_slabs = response_rate.reshape(slabs, TILE_DEV, PT)
    place_slabs = spanwise_position.reshape(slabs, TILE_DEV, PT)
    motion_slabs = jnp.moveaxis(particle_velocity.reshape(3, slabs, TILE_DEV, PT), 1, 0)
    seen_slabs = jnp.moveaxis(seen_velocity.reshape(3, slabs, TILE_DEV, PT), 1, 0)

    def slab_forcing(inputs):
        cell_slot, block_slot, amount, rate, place, motion, seen = inputs
        angles = place[..., None] * spanwise_waves
        phases = jnp.stack([jnp.cos(angles), -jnp.sin(angles)], axis=-2)
        drag_force = amount * rate * (seen - motion)
        amounts = jnp.moveaxis(jnp.concatenate([amount[None], drag_force], axis=0), 0, -1)
        payload = (amounts[..., :, None, None] * phases[..., None, :, :]).astype(jnp.bfloat16)
        payload = payload.reshape(TILE_DEV, PT, 8 * MZ).astype(jnp.float32)
        one_hot = (cell_slot[..., None] == lanes).astype(jnp.float32)
        shares = jnp.einsum('tpc,tpw->twc', one_hot, payload, precision=highest)
        totals = jnp.zeros((slab_rows * strips, 8 * MZ, CB), jnp.float32).at[block_slot].add(shares)
        field = totals.astype(jnp.bfloat16).astype(jnp.float32).reshape(slab_rows, strips, 8 * MZ, CB)
        product = jnp.einsum('ybwc,bcsi->ywsi', field, forward_float, precision=highest)
        product = product.reshape(slab_rows, 4, 2, MZ, 2, KX)
        real_part = product[:, :, 0, :, 0] + product[:, :, 1, :, 1]
        imag_part = product[:, :, 1, :, 0] - product[:, :, 0, :, 1]
        return jnp.stack([real_part, imag_part], axis=3).astype(jnp.bfloat16)
    forcing = lax.map(slab_forcing, (cell_slabs, block_slabs, volume_slabs, rate_slabs, place_slabs, motion_slabs, seen_slabs))
    forcing = forcing.reshape(NY, 4, MZ, 2, KX)
    stream_wave = (jnp.arange(KX) - KX // 2).astype(jnp.float32) * 0.5
    vertical = (jnp.arange(3) == 1).astype(jnp.float32)[None, :, None, None]

    def solve_mode(inputs):
        forcing_mode, state_mode, span_wave = inputs
        force = forcing_mode[:, 1:].astype(jnp.float32) - gravity * vertical * forcing_mode[:, :1].astype(jnp.float32)
        wave_square = stream_wave * stream_wave + span_wave * span_wave
        damping = 1.0 / (1.0 + viscosity * (eigenvalues[:, None, None, None] + wave_square[None, None, None, :]))
        modal = jnp.einsum('ij,jcrk->icrk', eigen_inverse, state_mode + time_step * force, precision=highest)
        return jnp.einsum('ij,jcrk->icrk', eigen_basis, modal * damping, precision=highest).astype(jnp.bfloat16)
    solved = lax.map(solve_mode, (jnp.moveaxis(forcing, 2, 0), jnp.moveaxis(fluid_velocity, 2, 0), spanwise_waves))
    solved = jnp.moveaxis(solved, 0, 2).reshape(slabs, slab_rows, 3, MZ, 2, KX)
    upward = (jnp.arange(3) == 1).astype(jnp.float32)[:, None, None]

    def slab_velocity(inputs):
        solved_slab, cell_slot, block_slot, rate, place, motion = inputs
        product = jnp.einsum('ycmri,isx->ycmrsx', solved_slab.astype(jnp.float32), inverse_float, precision=highest)
        real_part = product[:, :, :, 0, 0] - product[:, :, :, 1, 1]
        imag_part = product[:, :, :, 0, 1] + product[:, :, :, 1, 0]
        planes = jnp.stack([real_part, imag_part], axis=3).astype(jnp.bfloat16)
        block_view = planes.reshape(slab_rows, 6 * MZ, strips, CB)
        block_rows = block_view[block_slot // strips, :, block_slot % strips, :].astype(jnp.float32)
        one_hot = (cell_slot[..., None] == lanes).astype(jnp.float32)
        picked = jnp.einsum('tpc,twc->tpw', one_hot, block_rows, precision=highest).reshape(TILE_DEV, PT, 3, MZ, 2)
        angles = place[..., None] * spanwise_waves
        along = lax.optimization_barrier(jnp.sum(picked[..., 0] * jnp.cos(angles)[:, :, None, :] - picked[..., 1] * jnp.sin(angles)[:, :, None, :], axis=-1))
        fluid_at = jnp.moveaxis(along, -1, 0)
        updated = motion + time_step * rate * (fluid_at - motion) - time_step * gravity * upward
        return (planes, updated)
    planes, updated = lax.map(slab_velocity, (solved, cell_slabs, block_slabs, rate_slabs, place_slabs, motion_slabs))
    velocity_planes = planes.reshape(NY, 3, MZ, 2, NX)
    updated_velocity = jnp.moveaxis(updated, 0, 1).reshape(3, slabs * TILE_DEV, PT)
    return (velocity_planes, updated_velocity)
```

```python
import math

import jax
import jax.numpy as jnp
import ml_dtypes
import numpy as np
from jax import lax
from jax.experimental import pallas as pl
from jax.experimental.pallas import tpu as pltpu
from jax.sharding import PartitionSpec as P

NX = 2048
KX = 1024
NY = 512
CB = 256
PT = 512
TILES = 64
MODES = 8
ROWS = 8
STRIPS = 8
WIDTH = 3 * 2 * MODES
BLOCKS = ROWS * STRIPS
FOLD = NX // 4
KEPT = KX // 4
N_PX = 8
N_PZ = 8
SLABS = N_PX * N_PZ
TURN = 1.0 / (2.0 * math.pi)
COSINE = (
    1.0,
    -19.73920440673828,
    64.93911743164062,
    -85.45011138916016,
    60.16743087768555,
    -25.96688461303711,
    6.527706146240234,
)

time_step = 0.5
gravity = 0.8
viscosity = 0.0001

f32 = jnp.float32
bf16 = jnp.bfloat16
VMEM = pl.BlockSpec(memory_space=pltpu.VMEM)
SMEM = pl.BlockSpec(memory_space=pltpu.SMEM)
ANY = pl.BlockSpec(memory_space=pl.ANY)


def wave_tables():
    x = np.arange(FOLD, dtype=np.int64)[None, :, None]
    k = (
        4 * np.arange(KEPT, dtype=np.int64)[None, None, :]
        + np.arange(4, dtype=np.int64)[:, None, None]
        - KX // 2
    )
    angle = np.mod(k * x, NX) * (2.0 * math.pi / NX)
    table = np.stack([np.cos(angle), np.sin(angle)], axis=1) / math.sqrt(NX)
    return table.astype(np.float32).astype(ml_dtypes.bfloat16)


def lane_order():
    perm = np.zeros((128, 128), np.float32)
    lanes = np.arange(128)
    perm[4 * (lanes % 32) + lanes // 32, lanes] = 1.0
    return np.concatenate([perm, perm], axis=0).astype(ml_dtypes.bfloat16)


def cosine_turns(turns):
    part = turns - jnp.round(turns)
    square = part * part
    value = jnp.full_like(square, COSINE[-1])
    for term in COSINE[-2::-1]:
        value = value * square + term
    return value


def one_hot_cells(cell_row):
    cells = jnp.broadcast_to(cell_row.astype(f32), (16, PT)).astype(bf16)
    lines = lax.broadcasted_iota(jnp.int32, (16, PT), 0).astype(f32).astype(bf16)
    one, zero = jnp.ones((16, PT), bf16), jnp.zeros((16, PT), bf16)
    return jnp.concatenate(
        [jnp.where(cells == lines + jnp.asarray(16 * i, bf16), one, zero) for i in range(16)],
        axis=0,
    )


def mode_turns(group):
    line = lax.broadcasted_iota(jnp.int32, (16, PT), 0)
    wave = (group * MODES + line // 2 + 1).astype(f32)
    shift = (line % 2).astype(f32) * 0.25
    return wave, shift


def swap_lanes(parts):
    return [
        jnp.concatenate([part[:, 32 * i : 32 * i + 32] for part in parts], axis=1)
        for i in range(4)
    ]


def dot(a, b):
    return lax.dot_general(a, b, (((1,), (0,)), ((), ())), preferred_element_type=f32)


def dot_t(a, b):
    return lax.dot_general(a, b, (((1,), (1,)), ((), ())), preferred_element_type=f32)


def deposit_kernel(block, cell, volume, rate, place, motion, seen, folded, totals):
    group = lax.axis_index("grp")
    wave, shift = mode_turns(group)
    totals[...] = jnp.zeros_like(totals)

    def eight_tiles(turn, carry):
        first = pl.multiple_of(turn * 8, 8)
        here = pl.ds(first, 8)
        cells = cell[here, :]
        amount = volume[here, :]
        scale = amount * rate[here, :]
        angle = place[here, :] * TURN
        drags = [scale * (seen[c, here, :] - motion[c, here, :]) for c in range(3)]
        drags[1] = drags[1] - gravity * amount
        for i in range(8):
            phase = cosine_turns(
                wave * jnp.broadcast_to(angle[i : i + 1, :], (16, PT)) + shift
            )
            payload = jnp.concatenate(
                [
                    (phase * jnp.broadcast_to(drags[c][i : i + 1, :], (16, PT))).astype(bf16)
                    for c in range(3)
                ],
                axis=0,
            )
            shares = dot_t(payload, one_hot_cells(cells[i : i + 1, :]))
            target = pl.ds(pl.multiple_of(block[first + i] * WIDTH, WIDTH), WIDTH)
            for h in range(2):
                totals[h, target, :] += shares[:, 128 * h : 128 * h + 128]
        return carry

    lax.fori_loop(0, TILES // 8, eight_tiles, 0)

    def fold(index, carry):
        c = index // MODES
        m = index % MODES
        for h in range(2):
            for s in range(2):
                field = [
                    [
                        totals[
                            h,
                            pl.ds(
                                (s + 2 * j) * WIDTH + c * 16 + m * 2 + z,
                                ROWS,
                                stride=STRIPS * WIDTH,
                            ),
                            :,
                        ]
                        for z in range(2)
                    ]
                    for j in range(4)
                ]
                re = [field[j][0] for j in range(4)]
                im = [field[j][1] for j in range(4)]
                sums = (re[0] + re[2], im[0] + im[2])
                others = (re[1] + re[3], im[1] + im[3])
                lefts = (re[0] - re[2], im[0] - im[2])
                rights = (re[1] - re[3], im[1] - im[3])
                results = (
                    (sums[0] + others[0], sums[1] + others[1]),
                    (lefts[0] + rights[1], lefts[1] - rights[0]),
                    (sums[0] - others[0], sums[1] - others[1]),
                    (lefts[0] - rights[1], lefts[1] + rights[0]),
                )
                for q in range(4):
                    pair = jnp.concatenate(results[q], axis=0)
                    lanes = slice(s * 256 + h * 128, s * 256 + h * 128 + 128)
                    folded[q, c, m, :, lanes] = pair.astype(bf16)
        return carry

    lax.fori_loop(0, 3 * MODES, fold, 0)


def flow_kernel(
    folded,
    block,
    cell,
    rate,
    place,
    motion,
    tables,
    order,
    fluid_any,
    basis_any,
    inverse_any,
    eigenvalues,
    planes_out,
    updated,
    fluid,
    basis,
    inverse,
    split_basis,
    split_inverse,
    damping,
    ordered,
    forward_send,
    forward_recv,
    back_send,
    back_recv,
    planes,
    blocks,
    part,
    part_send,
    part_recv,
    load_sem,
    own_sem,
    send_sem,
    recv_sem,
    part_send_sem,
    part_recv_sem,
):
    grp = lax.axis_index("grp")
    px = lax.axis_index("px")
    pz = lax.axis_index("pz")
    me = px * N_PZ + pz

    def peer(step):
        return lax.rem(px + step // N_PZ, N_PX), lax.rem(pz + lax.rem(step, N_PZ), N_PZ)

    barrier = pltpu.get_barrier_semaphore()

    def greet(step, carry):
        a, b = peer(step)
        pl.semaphore_signal(barrier, inc=1, device_id={"px": a, "pz": b})
        return carry

    loads = [
        pltpu.make_async_copy(fluid_any, fluid, load_sem.at[0]),
        pltpu.make_async_copy(basis_any, basis, load_sem.at[1]),
        pltpu.make_async_copy(inverse_any, inverse, load_sem.at[2]),
    ]
    for load in loads:
        load.start()
    pl.semaphore_signal(barrier, inc=1, device_id={"grp": 1 - grp})
    lax.fori_loop(1, SLABS, greet, 0)

    def forward(c):
        classes = []
        for q in range(4):
            rows = folded[q, c].reshape(MODES * 16, FOLD)
            even = dot(rows, tables[q, 0]).reshape(MODES, 2, ROWS, KEPT)
            odd = dot(rows, tables[q, 1]).reshape(MODES, 2, ROWS, KEPT)
            re = even[:, 0] + odd[:, 1]
            im = even[:, 1] - odd[:, 0]
            classes.append(
                jnp.concatenate([re, im], axis=1).reshape(MODES * 16, KEPT)
            )
        for h in range(2):
            chunks = swap_lanes([item[:, 128 * h : 128 * h + 128] for item in classes])
            for i in range(4):
                first = (4 * h + i) * 128
                forward_send[c, :, :, first : first + 128] = (
                    chunks[i].astype(bf16).reshape(MODES, 16, 128)
                )

    def forward_start(c):
        def send(step, carry):
            a, b = peer(step)
            pltpu.make_async_remote_copy(
                forward_send.at[c, b, :, pl.ds(pl.multiple_of(a * 128, 128), 128)],
                forward_recv.at[c, me],
                send_sem.at[c],
                recv_sem.at[c],
                device_id={"px": a, "pz": b},
            ).start()
            return carry

        pltpu.make_async_copy(
            forward_send.at[c, pz, :, pl.ds(pl.multiple_of(px * 128, 128), 128)],
            forward_recv.at[c, me],
            own_sem.at[c],
        ).start()
        lax.fori_loop(1, SLABS, send, 0)

    def back_start(c):
        def send(step, carry):
            a, b = peer(step)
            pltpu.make_async_remote_copy(
                back_send.at[c, a * N_PZ + b],
                back_recv.at[c, pz, :, pl.ds(pl.multiple_of(px * 128, 128), 128)],
                send_sem.at[3 + c],
                recv_sem.at[3 + c],
                device_id={"px": a, "pz": b},
            ).start()
            return carry

        pltpu.make_async_copy(
            back_send.at[c, me],
            back_recv.at[c, pz, :, pl.ds(pl.multiple_of(px * 128, 128), 128)],
            own_sem.at[3 + c],
        ).start()
        lax.fori_loop(1, SLABS, send, 0)

    def exchange_wait(index):
        blocks = forward_recv.at[0, pl.ds(0, SLABS - 1)]
        pltpu.make_async_remote_copy(
            blocks,
            blocks,
            send_sem.at[index],
            recv_sem.at[index],
            device_id={"px": px, "pz": pz},
        ).wait_recv()
        own = forward_recv.at[0, 0]
        pltpu.make_async_copy(own, own, own_sem.at[index]).wait()

    def sent_wait(index):
        blocks = forward_recv.at[0, pl.ds(0, SLABS - 1)]
        pltpu.make_async_remote_copy(
            blocks,
            blocks,
            send_sem.at[index],
            recv_sem.at[index],
            device_id={"px": px, "pz": pz},
        ).wait_send()

    forward(0)
    pl.semaphore_wait(barrier, SLABS)
    forward_start(0)
    forward(1)
    forward_start(1)
    forward(2)
    forward_start(2)

    for load in loads:
        load.wait()
    for matrix, split in ((basis, split_basis), (inverse, split_inverse)):
        high = matrix[...].astype(bf16)
        split[0] = high
        split[1] = (matrix[...] - high.astype(f32)).astype(bf16)
    lane = lax.broadcasted_iota(jnp.int32, (1, 128), 1)
    wave = px * 128 + 4 * (lane % 32) + lane // 32 - KX // 2
    wave = wave.astype(f32) * 0.5
    span = (grp * MODES + pz + 1).astype(f32)
    square = wave * wave + span * span
    column = jnp.transpose(jnp.broadcast_to(eigenvalues[...], (128, NY)))
    damping[...] = 1.0 / (1.0 + viscosity * (column + square))
    for c in range(3):
        for r in range(2):
            state = fluid[pl.ds(c * 2 + r, NY, stride=6), :]
            high = state.astype(bf16)
            low = (state - high.astype(f32)).astype(bf16)
            ordered[c, :, 128 * r : 128 * r + 128] = dot(
                jnp.concatenate([high, low], axis=1), order[...]
            )

    def apply(split, value):
        high = value.astype(bf16)
        low = (value - high.astype(f32)).astype(bf16)
        return dot(split[0], high) + (dot(split[0], low) + dot(split[1], high))

    for c in range(3):
        exchange_wait(c)
        forcing = forward_recv[c].astype(f32)
        force = jnp.concatenate(
            [forcing[:, 8 * r : 8 * r + 8, :].reshape(NY, 128) for r in range(2)], axis=1
        )
        modal = apply(split_inverse, ordered[c] + time_step * force)
        damp = damping[...]
        solved = apply(split_basis, modal * jnp.concatenate([damp, damp], axis=1))
        back_send[c] = jnp.concatenate(
            [solved[:, 128 * r : 128 * r + 128].reshape(SLABS, ROWS, 128) for r in range(2)],
            axis=1,
        ).astype(bf16)
        back_start(c)

    def backward(c):
        halves = []
        for h in range(2):
            parts = [
                back_recv[c, :, :, (4 * h + i) * 128 : (4 * h + i) * 128 + 128].reshape(
                    MODES * 16, 128
                )
                for i in range(4)
            ]
            halves.append(swap_lanes(parts))
        re, im = [], []
        for q in range(4):
            rows = jnp.concatenate([halves[0][q], halves[1][q]], axis=1)
            even = dot_t(rows, tables[q, 0]).reshape(MODES, 2, ROWS, FOLD)
            odd = dot_t(rows, tables[q, 1]).reshape(MODES, 2, ROWS, FOLD)
            re.append(even[:, 0] - odd[:, 1])
            im.append(odd[:, 0] + even[:, 1])
        sums = (re[0] + re[2], im[0] + im[2])
        lefts = (re[0] - re[2], im[0] - im[2])
        others = (re[1] + re[3], im[1] + im[3])
        rights = (im[3] - im[1], re[1] - re[3])
        results = (
            (sums[0] + others[0], sums[1] + others[1]),
            (lefts[0] + rights[0], lefts[1] + rights[1]),
            (sums[0] - others[0], sums[1] - others[1]),
            (lefts[0] - rights[0], lefts[1] - rights[1]),
        )
        for j in range(4):
            for r in range(2):
                for m in range(MODES):
                    for s in range(2):
                        for h in range(2):
                            lanes = slice(s * 256 + h * 128, s * 256 + h * 128 + 128)
                            planes[
                                h,
                                pl.ds(
                                    (2 * j + s) * WIDTH + c * 16 + m * 2 + r,
                                    ROWS,
                                    stride=STRIPS * WIDTH,
                                ),
                                :,
                            ] = results[j][r][m, :, lanes]

    for c in range(3):
        exchange_wait(3 + c)
        backward(c)

    def write_row(y, carry):
        for s in range(STRIPS):
            source = pl.ds(pl.multiple_of((y * STRIPS + s) * WIDTH, WIDTH), WIDTH)
            for h in range(2):
                value = planes[h, source, :].astype(bf16)
                lanes = slice(s * 256 + h * 128, s * 256 + h * 128 + 128)
                planes_out[y, :, lanes] = value
                blocks[y * STRIPS + s, :, 128 * h : 128 * h + 128] = value
        return carry

    lax.fori_loop(0, ROWS, write_row, 0)

    wave, shift = mode_turns(grp)

    def part_copy(turn):
        here = pl.ds(pl.multiple_of(turn * 16, 16), 16)
        return pltpu.make_async_remote_copy(
            part_send.at[:, here, :],
            part_recv.at[:, here, :],
            part_send_sem.at[turn],
            part_recv_sem.at[turn],
            device_id={"grp": 1 - grp},
        )

    def sixteen_tiles(turn, carry):
        for half in range(2):
            first = pl.multiple_of(turn * 16 + 8 * half, 8)
            here = pl.ds(first, 8)
            cells = cell[here, :]
            angle = place[here, :] * TURN
            lines = [[], [], []]
            for i in range(8):
                phase = cosine_turns(
                    wave * jnp.broadcast_to(angle[i : i + 1, :], (16, PT)) + shift
                )
                picked = dot(blocks[block[first + i]], one_hot_cells(cells[i : i + 1, :]))
                for c in range(3):
                    lines[c].append(
                        jnp.sum(picked[16 * c : 16 * c + 16, :] * phase, axis=0, keepdims=True)
                    )
            for c in range(3):
                part[c, here, :] = jnp.concatenate(lines[c], axis=0)
        here = pl.ds(pl.multiple_of(turn * 16, 16), 16)
        for c in range(3):
            part_send[c, here, :] = part[c, here, :].astype(bf16)
        part_copy(turn).start()
        return carry

    lax.fori_loop(0, TILES // 16, sixteen_tiles, 0)

    def update(turn, carry):
        part_copy(turn).wait()
        here = pl.ds(pl.multiple_of(turn * 16, 16), 16)
        for c in range(3):
            fluid_at = part_send[c, here, :].astype(f32) + part_recv[c, here, :].astype(f32)
            old = motion[c, here, :]
            new = old + time_step * rate[here, :] * (fluid_at - old)
            updated[c, here, :] = new - time_step * gravity if c == 1 else new
        return carry

    lax.fori_loop(0, TILES // 16, update, 0)
    for index in range(6):
        sent_wait(index)


def on_device(
    cell_index,
    block_index,
    volume,
    response_rate,
    spanwise_position,
    particle_velocity,
    seen_velocity,
    fluid_velocity,
    eigen_basis,
    eigen_inverse,
    eigenvalues,
):
    folded = pl.pallas_call(
        deposit_kernel,
        out_shape=jax.ShapeDtypeStruct((4, 3, MODES, 16, FOLD), bf16),
        in_specs=[SMEM] + [VMEM] * 6,
        out_specs=VMEM,
        scratch_shapes=[pltpu.VMEM((2, BLOCKS * WIDTH, 128), f32)],
        compiler_params=pltpu.CompilerParams(vmem_limit_bytes=40 * 2**20),
        name="deposit",
    )(
        block_index,
        cell_index,
        volume,
        response_rate,
        spanwise_position,
        particle_velocity,
        seen_velocity,
    )
    tables = jnp.asarray(wave_tables())
    order = jnp.asarray(lane_order())
    planes, updated = pl.pallas_call(
        flow_kernel,
        out_shape=(
            jax.ShapeDtypeStruct((ROWS, WIDTH, NX), bf16),
            jax.ShapeDtypeStruct((3, TILES, PT), f32),
        ),
        in_specs=[VMEM, SMEM] + [VMEM] * 6 + [ANY] * 3 + [VMEM],
        out_specs=(VMEM, VMEM),
        scratch_shapes=[
            pltpu.VMEM((NY * 6, 128), f32),
            pltpu.VMEM((NY, NY), f32),
            pltpu.VMEM((NY, NY), f32),
            pltpu.VMEM((2, NY, NY), bf16),
            pltpu.VMEM((2, NY, NY), bf16),
            pltpu.VMEM((NY, 128), f32),
            pltpu.VMEM((3, NY, 256), f32),
            pltpu.VMEM((3, MODES, 16, KX), bf16),
            pltpu.VMEM((3, SLABS, 16, 128), bf16),
            pltpu.VMEM((3, SLABS, 16, 128), bf16),
            pltpu.VMEM((3, MODES, 16, KX), bf16),
            pltpu.VMEM((2, BLOCKS * WIDTH, 128), f32),
            pltpu.VMEM((BLOCKS, WIDTH, CB), bf16),
            pltpu.VMEM((3, TILES, PT), f32),
            pltpu.VMEM((3, TILES, PT), bf16),
            pltpu.VMEM((3, TILES, PT), bf16),
            pltpu.SemaphoreType.DMA((3,)),
            pltpu.SemaphoreType.DMA((6,)),
            pltpu.SemaphoreType.DMA((6,)),
            pltpu.SemaphoreType.DMA((6,)),
            pltpu.SemaphoreType.DMA((TILES // 16,)),
            pltpu.SemaphoreType.DMA((TILES // 16,)),
        ],
        compiler_params=pltpu.CompilerParams(
            collective_id=0, has_side_effects=True, vmem_limit_bytes=56 * 2**20
        ),
        name="flow",
    )(
        folded,
        block_index,
        cell_index,
        response_rate,
        spanwise_position,
        particle_velocity,
        tables,
        order,
        fluid_velocity.reshape(NY * 6, 128),
        eigen_basis,
        eigen_inverse,
        eigenvalues.reshape(1, NY),
    )
    return planes.reshape(ROWS, 3, MODES, 2, NX), updated


def solution(mesh):
    in_specs = (
        P(("px", "pz"), None),
        P(("px", "pz")),
        P(("px", "pz"), None),
        P(("px", "pz"), None),
        P(("px", "pz"), None),
        P(None, ("px", "pz"), None),
        P(None, ("px", "pz"), None),
        P(None, None, ("grp", "pz"), None, "px"),
        P(),
        P(),
        P(),
    )
    out_specs = (P(("px", "pz"), None, "grp", None, None), P(None, ("px", "pz"), None))
    return jax.shard_map(
        on_device, mesh=mesh, in_specs=in_specs, out_specs=out_specs, check_vma=False
    )
```

```python
import math

import jax
import jax.numpy as jnp
import ml_dtypes
import numpy as np
from jax import lax
from jax.experimental import pallas as pl
from jax.experimental.pallas import tpu as pltpu
from jax.sharding import PartitionSpec as P

NX = 2048
KX = 1024
NY = 512
CB = 256
PT = 512
TILES = 64
MODES = 8
ROWS = 8
STRIPS = 8
WIDTH = 3 * 2 * MODES
BLOCKS = ROWS * STRIPS
FOLD = NX // 4
KEPT = KX // 4
N_PX = 8
N_PZ = 8
SLABS = N_PX * N_PZ
TURN = 1.0 / (2.0 * math.pi)
COSINE = (
    1.0,
    -19.73920440673828,
    64.93911743164062,
    -85.45011138916016,
    60.16743087768555,
    -25.96688461303711,
    6.527706146240234,
)

time_step = 0.5
gravity = 0.8
viscosity = 0.0001

f32 = jnp.float32
bf16 = jnp.bfloat16
VMEM = pl.BlockSpec(memory_space=pltpu.VMEM)
SMEM = pl.BlockSpec(memory_space=pltpu.SMEM)
ANY = pl.BlockSpec(memory_space=pl.ANY)


def wave_tables():
    x = np.arange(FOLD, dtype=np.int64)[None, :, None]
    k = (
        4 * np.arange(KEPT, dtype=np.int64)[None, None, :]
        + np.arange(4, dtype=np.int64)[:, None, None]
        - KX // 2
    )
    angle = np.mod(k * x, NX) * (2.0 * math.pi / NX)
    table = np.stack([np.cos(angle), np.sin(angle)], axis=1) / math.sqrt(NX)
    return table.astype(np.float32).astype(ml_dtypes.bfloat16)


def lane_order():
    perm = np.zeros((128, 128), np.float32)
    lanes = np.arange(128)
    perm[4 * (lanes % 32) + lanes // 32, lanes] = 1.0
    return np.concatenate([perm, perm], axis=0).astype(ml_dtypes.bfloat16)


def cosine_turns(turns):
    part = turns - jnp.round(turns)
    square = part * part
    value = jnp.full_like(square, COSINE[-1])
    for term in COSINE[-2::-1]:
        value = value * square + term
    return value


def one_hot_cells(cell_row):
    cells = jnp.broadcast_to(cell_row.astype(f32), (16, PT)).astype(bf16)
    lines = lax.broadcasted_iota(jnp.int32, (16, PT), 0).astype(f32).astype(bf16)
    one, zero = jnp.ones((16, PT), bf16), jnp.zeros((16, PT), bf16)
    return jnp.concatenate(
        [jnp.where(cells == lines + jnp.asarray(16 * i, bf16), one, zero) for i in range(16)],
        axis=0,
    )


def mode_turns(group):
    line = lax.broadcasted_iota(jnp.int32, (16, PT), 0)
    wave = (group * MODES + line % 8 + 1).astype(f32)
    shift = (line // 8).astype(f32) * 0.25
    return wave, shift


def swap_lanes(parts):
    return [
        jnp.concatenate([part[:, 32 * i : 32 * i + 32] for part in parts], axis=1)
        for i in range(4)
    ]


def dot(a, b):
    return lax.dot_general(a, b, (((1,), (0,)), ((), ())), preferred_element_type=f32)


def dot_t(a, b):
    return lax.dot_general(a, b, (((1,), (1,)), ((), ())), preferred_element_type=f32)


def block_fold(blocks_line):
    rows = lax.broadcasted_iota(jnp.int32, (128, 256), 0)
    lanes = lax.broadcasted_iota(jnp.int32, (128, 256), 1)
    q, s, r, y = rows // 32, (rows // 16) % 2, (rows // 8) % 2, rows % 8
    z = (lanes // TILES) % 2
    tile_block = jnp.broadcast_to(
        jnp.concatenate([blocks_line] * 4, axis=1), (128, 256)
    )
    strip = tile_block & 7
    turn = (q * (strip >> 1) + r - z + 4) & 3
    value = jnp.where(turn == 0, 1.0, jnp.where(turn == 2, -1.0, 0.0))
    here = ((tile_block >> 3) == y) & ((strip & 1) == s)
    return jnp.where(here, value, 0.0).astype(bf16)


def flow_kernel(
    block,
    block_line,
    eigenvalues,
    cell_any,
    place_any,
    volume_any,
    rate_any,
    motion_any,
    seen_any,
    tables_any,
    order_any,
    fluid_any,
    basis_any,
    inverse_any,
    planes_any,
    updated_any,
    cell,
    place,
    volume,
    rate,
    motion,
    seen,
    tables,
    order,
    fluid,
    basis,
    inverse,
    shares,
    folded,
    cell_hot,
    phases,
    split_basis,
    split_inverse,
    damping,
    ordered,
    forward_send,
    forward_recv,
    back_send,
    back_recv,
    planes,
    planes_out,
    blocks,
    part,
    part_send,
    part_recv,
    updated,
    load_sem,
    store_sem,
    own_sem,
    send_sem,
    recv_sem,
    part_send_sem,
    part_recv_sem,
):
    grp = lax.axis_index("grp")
    px = lax.axis_index("px")
    pz = lax.axis_index("pz")
    me = px * N_PZ + pz

    def peer(step):
        return lax.rem(px + step // N_PZ, N_PX), lax.rem(pz + lax.rem(step, N_PZ), N_PZ)

    sources = (cell_any, place_any, volume_any, rate_any, motion_any, seen_any)
    sources += (tables_any, order_any, fluid_any, basis_any, inverse_any)
    targets = (cell, place, volume, rate, motion, seen)
    targets += (tables, order, fluid, basis, inverse)
    loads = [
        pltpu.make_async_copy(source, target, load_sem.at[i])
        for i, (source, target) in enumerate(zip(sources, targets))
    ]
    for load in loads:
        load.start()

    barrier = pltpu.get_barrier_semaphore()

    def greet(step, carry):
        a, b = peer(step)
        pl.semaphore_signal(barrier, inc=1, device_id={"px": a, "pz": b})
        return carry

    pl.semaphore_signal(barrier, inc=1, device_id={"grp": 1 - grp})
    lax.fori_loop(1, SLABS, greet, 0)

    selection = block_fold(block_line[...])
    wave, shift = mode_turns(grp)
    for load in loads[:6]:
        load.wait()

    def deposit(turn, carry):
        first = pl.multiple_of(turn * 8, 8)
        here = pl.ds(first, 8)
        cells = cell[here, :]
        amount = volume[here, :]
        scale = amount * rate[here, :]
        angle = place[here, :] * TURN
        drags = [scale * (seen[c, here, :] - motion[c, here, :]) for c in range(3)]
        drags[1] = drags[1] - gravity * amount
        for i in range(8):
            phase = cosine_turns(
                wave * jnp.broadcast_to(angle[i : i + 1, :], (16, PT)) + shift
            )
            phases[first + i] = phase
            payload = jnp.concatenate(
                [
                    (phase * jnp.broadcast_to(drags[c][i : i + 1, :], (16, PT))).astype(bf16)
                    for c in range(3)
                ],
                axis=0,
            )
            share = dot_t(payload, one_hot_cells(cells[i : i + 1, :]))
            target = pl.ds(pl.multiple_of((first + i) * WIDTH, WIDTH), WIDTH)
            for h in range(2):
                shares[h, target, :] = share[:, 128 * h : 128 * h + 128]
        return carry

    lax.fori_loop(0, TILES // 8, deposit, 0)

    def fold(c):
        for m in range(MODES):
            high, low = [], []
            for z in range(2):
                halves = [
                    shares[h, pl.ds(c * 16 + z * 8 + m, TILES, stride=WIDTH), :]
                    for h in range(2)
                ]
                value = jnp.concatenate(halves, axis=1)
                top = value.astype(bf16)
                high.append(top)
                low.append((value - top.astype(f32)).astype(bf16))
            sums = dot(selection, jnp.concatenate(high + low, axis=0))
            for q in range(4):
                for s in range(2):
                    first = q * 32 + s * 16
                    folded[q, m * 16 : m * 16 + 16, 256 * s : 256 * s + 256] = sums[
                        first : first + 16, :
                    ].astype(bf16)

    def forward(c):
        classes = []
        for q in range(4):
            even = dot(folded[q], tables[q, 0]).reshape(MODES, 2, ROWS, KEPT)
            odd = dot(folded[q], tables[q, 1]).reshape(MODES, 2, ROWS, KEPT)
            re = even[:, 0] + odd[:, 1]
            im = even[:, 1] - odd[:, 0]
            classes.append(
                jnp.concatenate([re, im], axis=1).reshape(MODES * 16, KEPT)
            )
        for h in range(2):
            chunks = swap_lanes([item[:, 128 * h : 128 * h + 128] for item in classes])
            for i in range(4):
                first = (4 * h + i) * 128
                forward_send[c, :, :, first : first + 128] = (
                    chunks[i].astype(bf16).reshape(MODES, 16, 128)
                )

    def forward_start(c):
        def send(step, carry):
            a, b = peer(step)
            pltpu.make_async_remote_copy(
                forward_send.at[c, b, :, pl.ds(pl.multiple_of(a * 128, 128), 128)],
                forward_recv.at[c, me],
                send_sem.at[c],
                recv_sem.at[c],
                device_id={"px": a, "pz": b},
            ).start()
            return carry

        pltpu.make_async_copy(
            forward_send.at[c, pz, :, pl.ds(pl.multiple_of(px * 128, 128), 128)],
            forward_recv.at[c, me],
            own_sem.at[c],
        ).start()
        lax.fori_loop(1, SLABS, send, 0)

    def back_start(c):
        def send(step, carry):
            a, b = peer(step)
            pltpu.make_async_remote_copy(
                back_send.at[c, a * N_PZ + b],
                back_recv.at[c, pz, :, pl.ds(pl.multiple_of(px * 128, 128), 128)],
                send_sem.at[3 + c],
                recv_sem.at[3 + c],
                device_id={"px": a, "pz": b},
            ).start()
            return carry

        pltpu.make_async_copy(
            back_send.at[c, me],
            back_recv.at[c, pz, :, pl.ds(pl.multiple_of(px * 128, 128), 128)],
            own_sem.at[3 + c],
        ).start()
        lax.fori_loop(1, SLABS, send, 0)

    def exchange_wait(index):
        blocks_in = forward_recv.at[0, pl.ds(0, SLABS - 1)]
        pltpu.make_async_remote_copy(
            blocks_in,
            blocks_in,
            send_sem.at[index],
            recv_sem.at[index],
            device_id={"px": px, "pz": pz},
        ).wait_recv()
        own = forward_recv.at[0, 0]
        pltpu.make_async_copy(own, own, own_sem.at[index]).wait()

    def sent_wait(index):
        blocks_out = forward_recv.at[0, pl.ds(0, SLABS - 1)]
        pltpu.make_async_remote_copy(
            blocks_out,
            blocks_out,
            send_sem.at[index],
            recv_sem.at[index],
            device_id={"px": px, "pz": pz},
        ).wait_send()

    fold(0)
    for load in loads[6:]:
        load.wait()
    forward(0)
    pl.semaphore_wait(barrier, SLABS)
    forward_start(0)
    for c in range(1, 3):
        fold(c)
        forward(c)
        forward_start(c)

    for matrix, split in ((basis, split_basis), (inverse, split_inverse)):
        high = matrix[...].astype(bf16)
        split[0] = high
        split[1] = (matrix[...] - high.astype(f32)).astype(bf16)
    lane = lax.broadcasted_iota(jnp.int32, (1, 128), 1)
    stream = px * 128 + 4 * (lane % 32) + lane // 32 - KX // 2
    stream = stream.astype(f32) * 0.5
    span = (grp * MODES + pz + 1).astype(f32)
    square = stream * stream + span * span
    column = jnp.transpose(jnp.broadcast_to(eigenvalues[...], (128, NY)))
    damping[...] = 1.0 / (1.0 + viscosity * (column + square))
    for c in range(3):
        for r in range(2):
            state = fluid[pl.ds(c * 2 + r, NY, stride=6), :]
            high = state.astype(bf16)
            low = (state - high.astype(f32)).astype(bf16)
            ordered[c, :, 128 * r : 128 * r + 128] = dot(
                jnp.concatenate([high, low], axis=1), order[...]
            )

    def make_hot(turn, carry):
        first = pl.multiple_of(turn * 8, 8)
        cells = cell[pl.ds(first, 8), :]
        for i in range(8):
            cell_hot[first + i] = one_hot_cells(cells[i : i + 1, :])
        return carry

    lax.fori_loop(0, TILES // 8, make_hot, 0)

    def apply(split, value):
        high = value.astype(bf16)
        low = (value - high.astype(f32)).astype(bf16)
        return dot(split[0], high) + (dot(split[0], low) + dot(split[1], high))

    for c in range(3):
        exchange_wait(c)
        forcing = forward_recv[c].astype(f32)
        force = jnp.concatenate(
            [forcing[:, 8 * r : 8 * r + 8, :].reshape(NY, 128) for r in range(2)], axis=1
        )
        modal = apply(split_inverse, ordered[c] + time_step * force)
        damp = damping[...]
        solved = apply(split_basis, modal * jnp.concatenate([damp, damp], axis=1))
        back_send[c] = jnp.concatenate(
            [solved[:, 128 * r : 128 * r + 128].reshape(SLABS, ROWS, 128) for r in range(2)],
            axis=1,
        ).astype(bf16)
        back_start(c)

    def backward(c):
        halves = []
        for h in range(2):
            parts = [
                back_recv[c, :, :, (4 * h + i) * 128 : (4 * h + i) * 128 + 128].reshape(
                    MODES * 16, 128
                )
                for i in range(4)
            ]
            halves.append(swap_lanes(parts))
        re, im = [], []
        for q in range(4):
            rows = jnp.concatenate([halves[0][q], halves[1][q]], axis=1)
            even = dot_t(rows, tables[q, 0]).reshape(MODES, 2, ROWS, FOLD)
            odd = dot_t(rows, tables[q, 1]).reshape(MODES, 2, ROWS, FOLD)
            re.append(even[:, 0] - odd[:, 1])
            im.append(odd[:, 0] + even[:, 1])
        sums = (re[0] + re[2], im[0] + im[2])
        lefts = (re[0] - re[2], im[0] - im[2])
        others = (re[1] + re[3], im[1] + im[3])
        rights = (im[3] - im[1], re[1] - re[3])
        results = (
            (sums[0] + others[0], sums[1] + others[1]),
            (lefts[0] + rights[0], lefts[1] + rights[1]),
            (sums[0] - others[0], sums[1] - others[1]),
            (lefts[0] - rights[0], lefts[1] - rights[1]),
        )
        for j in range(4):
            for r in range(2):
                for m in range(MODES):
                    for t in range(4):
                        planes[
                            pl.ds(m * 32 + (4 * j + t) * 2 + r, ROWS, stride=MODES * 32), :
                        ] = results[j][r][m, :, 128 * t : 128 * t + 128]

        def one_row(y, carry):
            first = pl.multiple_of(y * MODES * 32, MODES * 32)
            planes_out[y, c] = planes[pl.ds(first, MODES * 32), :].astype(bf16)
            for s in range(STRIPS):
                for h in range(2):
                    pair = [
                        planes[pl.ds(first + (2 * s + h) * 2 + r, MODES, stride=32), :]
                        for r in range(2)
                    ]
                    blocks[c, y * STRIPS + s, :, 128 * h : 128 * h + 128] = jnp.concatenate(
                        pair, axis=0
                    ).astype(bf16)
            return carry

        lax.fori_loop(0, ROWS, one_row, 0)

    def part_copy(which, turn):
        c, count = (0, 2) if which == 0 else (2, 1)
        here = pl.ds(pl.multiple_of(turn * 16, 16), 16)
        return pltpu.make_async_remote_copy(
            part_send.at[pl.ds(c, count), here, :],
            part_recv.at[pl.ds(c, count), here, :],
            part_send_sem.at[which, turn],
            part_recv_sem.at[which, turn],
            device_id={"grp": 1 - grp},
        )

    def sample(which):
        components = (0, 1) if which == 0 else (2,)

        def sixteen_tiles(turn, carry):
            for half in range(2):
                first = pl.multiple_of(turn * 16 + 8 * half, 8)
                here = pl.ds(first, 8)
                lines = [[] for c in components]
                for i in range(8):
                    own_block = block[first + i]
                    rows = jnp.concatenate([blocks[c, own_block] for c in components], axis=0)
                    picked = dot(rows, cell_hot[first + i])
                    phase = phases[first + i]
                    for n in range(len(components)):
                        lines[n].append(
                            jnp.sum(
                                picked[16 * n : 16 * n + 16, :] * phase, axis=0, keepdims=True
                            )
                        )
                for n, c in enumerate(components):
                    part[c, here, :] = jnp.concatenate(lines[n], axis=0)
            here = pl.ds(pl.multiple_of(turn * 16, 16), 16)
            for c in components:
                part_send[c, here, :] = part[c, here, :].astype(bf16)
            part_copy(which, turn).start()
            return carry

        lax.fori_loop(0, TILES // 16, sixteen_tiles, 0)

    def update(which):
        components = (0, 1) if which == 0 else (2,)

        def sixteen_tiles(turn, carry):
            part_copy(which, turn).wait()
            here = pl.ds(pl.multiple_of(turn * 16, 16), 16)
            for c in components:
                fluid_at = part_send[c, here, :].astype(f32) + part_recv[c, here, :].astype(f32)
                old = motion[c, here, :]
                new = old + time_step * rate[here, :] * (fluid_at - old)
                updated[c, here, :] = new - time_step * gravity if c == 1 else new
            return carry

        lax.fori_loop(0, TILES // 16, sixteen_tiles, 0)

    stores = []

    def store(source, target):
        stores.append(pltpu.make_async_copy(source, target, store_sem.at[len(stores)]))
        stores[-1].start()

    exchange_wait(3)
    backward(0)
    store(planes_out.at[:, 0], planes_any.at[:, 0])
    exchange_wait(4)
    backward(1)
    store(planes_out.at[:, 1], planes_any.at[:, 1])
    sample(0)
    exchange_wait(5)
    backward(2)
    store(planes_out.at[:, 2], planes_any.at[:, 2])
    sample(1)
    update(0)
    store(updated.at[pl.ds(0, 2)], updated_any.at[pl.ds(0, 2)])
    update(1)
    store(updated.at[pl.ds(2, 1)], updated_any.at[pl.ds(2, 1)])
    for index in range(6):
        sent_wait(index)
    for item in stores:
        item.wait()


def on_device(
    cell_index,
    block_index,
    volume,
    response_rate,
    spanwise_position,
    particle_velocity,
    seen_velocity,
    fluid_velocity,
    eigen_basis,
    eigen_inverse,
    eigenvalues,
):
    tables = jnp.asarray(wave_tables())
    order = jnp.asarray(lane_order())
    particles = ((TILES, PT), f32)
    vectors = ((3, TILES, PT), f32)
    scratch = (
        ((TILES, PT), jnp.int32),
        particles,
        particles,
        particles,
        vectors,
        vectors,
        (tables.shape, bf16),
        (order.shape, bf16),
        ((NY * 6, 128), f32),
        ((NY, NY), f32),
        ((NY, NY), f32),
        ((2, TILES * WIDTH, 128), f32),
        ((4, MODES * 16, FOLD), bf16),
        ((TILES, CB, PT), bf16),
        ((TILES, 16, PT), f32),
        ((2, NY, NY), bf16),
        ((2, NY, NY), bf16),
        ((NY, 128), f32),
        ((3, NY, 256), f32),
        ((3, MODES, 16, KX), bf16),
        ((3, SLABS, 16, 128), bf16),
        ((3, SLABS, 16, 128), bf16),
        ((3, MODES, 16, KX), bf16),
        ((ROWS * MODES * 32, 128), f32),
        ((ROWS, 3, MODES * 32, 128), bf16),
        ((3, BLOCKS, 16, CB), bf16),
        vectors,
        ((3, TILES, PT), bf16),
        ((3, TILES, PT), bf16),
        vectors,
    )
    planes, updated = pl.pallas_call(
        flow_kernel,
        out_shape=(
            jax.ShapeDtypeStruct((ROWS, 3, MODES * 32, 128), bf16),
            jax.ShapeDtypeStruct((3, TILES, PT), f32),
        ),
        in_specs=[SMEM, VMEM, VMEM] + [ANY] * 11,
        out_specs=(ANY, ANY),
        scratch_shapes=[pltpu.VMEM(*item) for item in scratch]
        + [
            pltpu.SemaphoreType.DMA((11,)),
            pltpu.SemaphoreType.DMA((5,)),
            pltpu.SemaphoreType.DMA((6,)),
            pltpu.SemaphoreType.DMA((6,)),
            pltpu.SemaphoreType.DMA((6,)),
            pltpu.SemaphoreType.DMA((2, TILES // 16)),
            pltpu.SemaphoreType.DMA((2, TILES // 16)),
        ],
        compiler_params=pltpu.CompilerParams(
            collective_id=0, has_side_effects=True, vmem_limit_bytes=58 * 2**20
        ),
        name="flow",
    )(
        block_index,
        block_index.reshape(1, TILES),
        eigenvalues.reshape(1, NY),
        cell_index,
        spanwise_position,
        volume,
        response_rate,
        particle_velocity,
        seen_velocity,
        tables,
        order,
        fluid_velocity.reshape(NY * 6, 128),
        eigen_basis,
        eigen_inverse,
    )
    planes = planes.reshape(ROWS, 3, MODES, 16, 2, 128)
    planes = jnp.transpose(planes, (0, 1, 2, 4, 3, 5)).reshape(ROWS, 3, MODES, 2, NX)
    return planes, updated


def solution(mesh):
    in_specs = (
        P(("px", "pz"), None),
        P(("px", "pz")),
        P(("px", "pz"), None),
        P(("px", "pz"), None),
        P(("px", "pz"), None),
        P(None, ("px", "pz"), None),
        P(None, ("px", "pz"), None),
        P(None, None, ("grp", "pz"), None, "px"),
        P(),
        P(),
        P(),
    )
    out_specs = (P(("px", "pz"), None, "grp", None, None), P(None, ("px", "pz"), None))
    return jax.shard_map(
        on_device, mesh=mesh, in_specs=in_specs, out_specs=out_specs, check_vma=False
    )
```

```python
import math

import jax
import jax.numpy as jnp
import ml_dtypes
import numpy as np
from jax import lax
from jax.experimental import pallas as pl
from jax.experimental.pallas import tpu as pltpu
from jax.sharding import PartitionSpec as P

NX = 2048
KX = 1024
NY = 512
CB = 256
PT = 512
TILES = 64
MODES = 8
ROWS = 8
STRIPS = 8
WIDTH = 3 * 2 * MODES
BLOCKS = ROWS * STRIPS
FOLD = NX // 4
KEPT = KX // 4
N_PX = 8
N_PZ = 8
SLABS = N_PX * N_PZ
TURN = 1.0 / (2.0 * math.pi)
COSINE = (
    1.0,
    -19.73920440673828,
    64.93911743164062,
    -85.45011138916016,
    60.16743087768555,
    -25.96688461303711,
    6.527706146240234,
)

time_step = 0.5
gravity = 0.8
viscosity = 0.0001

f32 = jnp.float32
bf16 = jnp.bfloat16
VMEM = pl.BlockSpec(memory_space=pltpu.VMEM)
SMEM = pl.BlockSpec(memory_space=pltpu.SMEM)
ANY = pl.BlockSpec(memory_space=pl.ANY)


def wave_tables():
    x = np.arange(FOLD, dtype=np.int64)[None, :, None]
    k = (
        4 * np.arange(KEPT, dtype=np.int64)[None, None, :]
        + np.arange(4, dtype=np.int64)[:, None, None]
        - KX // 2
    )
    angle = np.mod(k * x, NX) * (2.0 * math.pi / NX)
    table = np.stack([np.cos(angle), np.sin(angle)], axis=1) / math.sqrt(NX)
    return table.astype(np.float32).astype(ml_dtypes.bfloat16)


def lane_order():
    perm = np.zeros((128, 128), np.float32)
    lanes = np.arange(128)
    perm[4 * (lanes % 32) + lanes // 32, lanes] = 1.0
    return np.concatenate([perm, perm], axis=0).astype(ml_dtypes.bfloat16)


def cosine_turns(turns):
    part = turns - jnp.round(turns)
    square = part * part
    value = jnp.full_like(square, COSINE[-1])
    for term in COSINE[-2::-1]:
        value = value * square + term
    return value


def one_hot_cells(cell_row):
    cells = jnp.broadcast_to((cell_row & 127).astype(f32), (16, PT)).astype(bf16)
    lines = lax.broadcasted_iota(jnp.int32, (16, PT), 0).astype(f32).astype(bf16)
    one, zero = jnp.ones((16, PT), bf16), jnp.zeros((16, PT), bf16)
    return jnp.concatenate(
        [jnp.where(cells == lines + jnp.asarray(16 * i, bf16), one, zero) for i in range(8)],
        axis=0,
    )


def mode_turns(group):
    line = lax.broadcasted_iota(jnp.int32, (16, PT), 0)
    wave = (group * MODES + line % 8 + 1).astype(f32)
    shift = (line // 8).astype(f32) * 0.25
    return wave, shift


def swap_lanes(parts):
    return [
        jnp.concatenate([part[:, 32 * i : 32 * i + 32] for part in parts], axis=1)
        for i in range(4)
    ]


def dot(a, b):
    return lax.dot_general(a, b, (((1,), (0,)), ((), ())), preferred_element_type=f32)


def dot_t(a, b):
    return lax.dot_general(a, b, (((1,), (1,)), ((), ())), preferred_element_type=f32)


def block_fold(blocks_line):
    rows = lax.broadcasted_iota(jnp.int32, (128, 256), 0)
    lanes = lax.broadcasted_iota(jnp.int32, (128, 256), 1)
    q, s, r, y = rows // 32, (rows // 16) % 2, (rows // 8) % 2, rows % 8
    z = (lanes // TILES) % 2
    tile_block = jnp.broadcast_to(
        jnp.concatenate([blocks_line] * 4, axis=1), (128, 256)
    )
    strip = tile_block & 7
    turn = (q * (strip >> 1) + r - z + 4) & 3
    value = jnp.where(turn == 0, 1.0, jnp.where(turn == 2, -1.0, 0.0))
    here = ((tile_block >> 3) == y) & ((strip & 1) == s)
    return jnp.where(here, value, 0.0).astype(bf16)


def flow_kernel(
    block,
    block_line,
    eigenvalues,
    cell_any,
    place_any,
    volume_any,
    rate_any,
    motion_any,
    seen_any,
    tables_any,
    order_any,
    fluid_any,
    basis_any,
    inverse_any,
    planes_any,
    updated_any,
    cell,
    place,
    volume,
    rate,
    motion,
    seen,
    tables,
    order,
    fluid,
    basis,
    inverse,
    shares,
    folded,
    phases,
    split_basis,
    split_inverse,
    damping,
    ordered,
    forward_send,
    forward_recv,
    back_send,
    back_recv,
    planes,
    planes_out,
    blocks,
    part,
    part_send,
    part_recv,
    updated,
    load_sem,
    store_sem,
    own_sem,
    send_sem,
    recv_sem,
    part_send_sem,
    part_recv_sem,
):
    grp = lax.axis_index("grp")
    px = lax.axis_index("px")
    pz = lax.axis_index("pz")
    me = px * N_PZ + pz

    def peer(step):
        return lax.rem(px + step // N_PZ, N_PX), lax.rem(pz + lax.rem(step, N_PZ), N_PZ)

    sources = (cell_any, place_any, volume_any, rate_any, motion_any, seen_any)
    sources += (tables_any, order_any, fluid_any, basis_any, inverse_any)
    targets = (cell, place, volume, rate, motion, seen)
    targets += (tables, order, fluid, basis, inverse)
    loads = [
        pltpu.make_async_copy(source, target, load_sem.at[i])
        for i, (source, target) in enumerate(zip(sources, targets))
    ]
    for load in loads:
        load.start()

    barrier = pltpu.get_barrier_semaphore()

    def greet(step, carry):
        a, b = peer(step)
        pl.semaphore_signal(barrier, inc=1, device_id={"px": a, "pz": b})
        return carry

    pl.semaphore_signal(barrier, inc=1, device_id={"grp": 1 - grp})
    lax.fori_loop(1, SLABS, greet, 0)

    selection = block_fold(block_line[...])
    wave, shift = mode_turns(grp)
    for load in loads[:6]:
        load.wait()

    def deposit(turn, carry):
        first = pl.multiple_of(turn * 8, 8)
        here = pl.ds(first, 8)
        cells = cell[here, :]
        amount = volume[here, :]
        scale = amount * rate[here, :]
        angle = place[here, :] * TURN
        drags = [scale * (seen[c, here, :] - motion[c, here, :]) for c in range(3)]
        drags[1] = drags[1] - gravity * amount
        for i in range(8):
            phase = cosine_turns(
                wave * jnp.broadcast_to(angle[i : i + 1, :], (16, PT)) + shift
            )
            phases[first + i] = phase
            below = jnp.broadcast_to(cells[i : i + 1, :], (16, PT)) < 128
            lower, upper = [], []
            for c in range(3):
                payload = phase * jnp.broadcast_to(drags[c][i : i + 1, :], (16, PT))
                lower.append(jnp.where(below, payload, 0.0).astype(bf16))
                upper.append(jnp.where(below, 0.0, payload).astype(bf16))
            share = dot_t(
                jnp.concatenate(lower + upper, axis=0), one_hot_cells(cells[i : i + 1, :])
            )
            target = pl.ds(pl.multiple_of((first + i) * WIDTH, WIDTH), WIDTH)
            for h in range(2):
                shares[h, target, :] = share[WIDTH * h : WIDTH * h + WIDTH, :]
        return carry

    lax.fori_loop(0, TILES // 8, deposit, 0)

    def fold(c):
        for m in range(MODES):
            high, low = [], []
            for z in range(2):
                halves = [
                    shares[h, pl.ds(c * 16 + z * 8 + m, TILES, stride=WIDTH), :]
                    for h in range(2)
                ]
                value = jnp.concatenate(halves, axis=1)
                top = value.astype(bf16)
                high.append(top)
                low.append((value - top.astype(f32)).astype(bf16))
            sums = dot(selection, jnp.concatenate(high + low, axis=0))
            for q in range(4):
                for s in range(2):
                    first = q * 32 + s * 16
                    folded[q, m * 16 : m * 16 + 16, 256 * s : 256 * s + 256] = sums[
                        first : first + 16, :
                    ].astype(bf16)

    def forward(c):
        classes = []
        for q in range(4):
            even = dot(folded[q], tables[q, 0]).reshape(MODES, 2, ROWS, KEPT)
            odd = dot(folded[q], tables[q, 1]).reshape(MODES, 2, ROWS, KEPT)
            re = even[:, 0] + odd[:, 1]
            im = even[:, 1] - odd[:, 0]
            classes.append(
                jnp.concatenate([re, im], axis=1).reshape(MODES * 16, KEPT)
            )
        for h in range(2):
            chunks = swap_lanes([item[:, 128 * h : 128 * h + 128] for item in classes])
            for i in range(4):
                first = (4 * h + i) * 128
                forward_send[c, :, :, first : first + 128] = (
                    chunks[i].astype(bf16).reshape(MODES, 16, 128)
                )

    def forward_start(c):
        def send(step, carry):
            a, b = peer(step)
            pltpu.make_async_remote_copy(
                forward_send.at[c, b, :, pl.ds(pl.multiple_of(a * 128, 128), 128)],
                forward_recv.at[c, me],
                send_sem.at[c],
                recv_sem.at[c],
                device_id={"px": a, "pz": b},
            ).start()
            return carry

        pltpu.make_async_copy(
            forward_send.at[c, pz, :, pl.ds(pl.multiple_of(px * 128, 128), 128)],
            forward_recv.at[c, me],
            own_sem.at[c],
        ).start()
        lax.fori_loop(1, SLABS, send, 0)

    def back_start(c):
        def send(step, carry):
            a, b = peer(step)
            pltpu.make_async_remote_copy(
                back_send.at[c, a * N_PZ + b],
                back_recv.at[c, pz, :, pl.ds(pl.multiple_of(px * 128, 128), 128)],
                send_sem.at[3 + c],
                recv_sem.at[3 + c],
                device_id={"px": a, "pz": b},
            ).start()
            return carry

        pltpu.make_async_copy(
            back_send.at[c, me],
            back_recv.at[c, pz, :, pl.ds(pl.multiple_of(px * 128, 128), 128)],
            own_sem.at[3 + c],
        ).start()
        lax.fori_loop(1, SLABS, send, 0)

    def exchange_wait(index):
        blocks_in = forward_recv.at[0, pl.ds(0, SLABS - 1)]
        pltpu.make_async_remote_copy(
            blocks_in,
            blocks_in,
            send_sem.at[index],
            recv_sem.at[index],
            device_id={"px": px, "pz": pz},
        ).wait_recv()
        own = forward_recv.at[0, 0]
        pltpu.make_async_copy(own, own, own_sem.at[index]).wait()

    def sent_wait(index):
        blocks_out = forward_recv.at[0, pl.ds(0, SLABS - 1)]
        pltpu.make_async_remote_copy(
            blocks_out,
            blocks_out,
            send_sem.at[index],
            recv_sem.at[index],
            device_id={"px": px, "pz": pz},
        ).wait_send()

    fold(0)
    for load in loads[6:]:
        load.wait()
    forward(0)
    pl.semaphore_wait(barrier, SLABS)
    forward_start(0)
    for c in range(1, 3):
        fold(c)
        forward(c)
        forward_start(c)

    for matrix, split in ((basis, split_basis), (inverse, split_inverse)):
        high = matrix[...].astype(bf16)
        split[0] = high
        split[1] = (matrix[...] - high.astype(f32)).astype(bf16)
    lane = lax.broadcasted_iota(jnp.int32, (1, 128), 1)
    stream = px * 128 + 4 * (lane % 32) + lane // 32 - KX // 2
    stream = stream.astype(f32) * 0.5
    span = (grp * MODES + pz + 1).astype(f32)
    square = stream * stream + span * span
    column = jnp.transpose(jnp.broadcast_to(eigenvalues[...], (128, NY)))
    damping[...] = 1.0 / (1.0 + viscosity * (column + square))
    for c in range(3):
        for r in range(2):
            state = fluid[pl.ds(c * 2 + r, NY, stride=6), :]
            high = state.astype(bf16)
            low = (state - high.astype(f32)).astype(bf16)
            ordered[c, :, 128 * r : 128 * r + 128] = dot(
                jnp.concatenate([high, low], axis=1), order[...]
            )

    def apply(split, value):
        high = value.astype(bf16)
        low = (value - high.astype(f32)).astype(bf16)
        return dot(split[0], high) + (dot(split[0], low) + dot(split[1], high))

    for c in range(3):
        exchange_wait(c)
        forcing = forward_recv[c].astype(f32)
        force = jnp.concatenate(
            [forcing[:, 8 * r : 8 * r + 8, :].reshape(NY, 128) for r in range(2)], axis=1
        )
        modal = apply(split_inverse, ordered[c] + time_step * force)
        damp = damping[...]
        solved = apply(split_basis, modal * jnp.concatenate([damp, damp], axis=1))
        back_send[c] = jnp.concatenate(
            [solved[:, 128 * r : 128 * r + 128].reshape(SLABS, ROWS, 128) for r in range(2)],
            axis=1,
        ).astype(bf16)
        back_start(c)

    def backward(c):
        halves = []
        for h in range(2):
            parts = [
                back_recv[c, :, :, (4 * h + i) * 128 : (4 * h + i) * 128 + 128].reshape(
                    MODES * 16, 128
                )
                for i in range(4)
            ]
            halves.append(swap_lanes(parts))
        re, im = [], []
        for q in range(4):
            rows = jnp.concatenate([halves[0][q], halves[1][q]], axis=1)
            even = dot_t(rows, tables[q, 0]).reshape(MODES, 2, ROWS, FOLD)
            odd = dot_t(rows, tables[q, 1]).reshape(MODES, 2, ROWS, FOLD)
            re.append(even[:, 0] - odd[:, 1])
            im.append(odd[:, 0] + even[:, 1])
        sums = (re[0] + re[2], im[0] + im[2])
        lefts = (re[0] - re[2], im[0] - im[2])
        others = (re[1] + re[3], im[1] + im[3])
        rights = (im[3] - im[1], re[1] - re[3])
        results = (
            (sums[0] + others[0], sums[1] + others[1]),
            (lefts[0] + rights[0], lefts[1] + rights[1]),
            (sums[0] - others[0], sums[1] - others[1]),
            (lefts[0] - rights[0], lefts[1] - rights[1]),
        )
        for j in range(4):
            for r in range(2):
                for m in range(MODES):
                    for t in range(4):
                        planes[
                            pl.ds(m * 32 + (4 * j + t) * 2 + r, ROWS, stride=MODES * 32), :
                        ] = results[j][r][m, :, 128 * t : 128 * t + 128]

        def one_row(y, carry):
            first = pl.multiple_of(y * MODES * 32, MODES * 32)
            planes_out[y, c] = planes[pl.ds(first, MODES * 32), :].astype(bf16)
            for s in range(STRIPS):
                for h in range(2):
                    pair = [
                        planes[pl.ds(first + (2 * s + h) * 2 + r, MODES, stride=32), :]
                        for r in range(2)
                    ]
                    blocks[c, y * STRIPS + s, :, 128 * h : 128 * h + 128] = jnp.concatenate(
                        pair, axis=0
                    ).astype(bf16)
            return carry

        lax.fori_loop(0, ROWS, one_row, 0)

    def part_copy(turn):
        here = pl.ds(pl.multiple_of(turn * 16, 16), 16)
        return pltpu.make_async_remote_copy(
            part_send.at[:, here, :],
            part_recv.at[:, here, :],
            part_send_sem.at[turn],
            part_recv_sem.at[turn],
            device_id={"grp": 1 - grp},
        )

    def sample(turn, carry):
        for half in range(2):
            first = pl.multiple_of(turn * 16 + 8 * half, 8)
            here = pl.ds(first, 8)
            cells = cell[here, :]
            lines = [[], [], []]
            for i in range(8):
                own_block = block[first + i]
                rows = [blocks[c, own_block] for c in range(3)]
                rows = jnp.concatenate(
                    [item[:, :128] for item in rows] + [item[:, 128:] for item in rows], axis=0
                )
                both = dot(rows, one_hot_cells(cells[i : i + 1, :]))
                below = jnp.broadcast_to(cells[i : i + 1, :], (WIDTH, PT)) < 128
                picked = jnp.where(below, both[:WIDTH], both[WIDTH:])
                phase = phases[first + i]
                for c in range(3):
                    lines[c].append(
                        jnp.sum(picked[16 * c : 16 * c + 16, :] * phase, axis=0, keepdims=True)
                    )
            for c in range(3):
                part[c, here, :] = jnp.concatenate(lines[c], axis=0)
        here = pl.ds(pl.multiple_of(turn * 16, 16), 16)
        for c in range(3):
            part_send[c, here, :] = part[c, here, :].astype(bf16)
        part_copy(turn).start()
        return carry

    def update(turn, carry):
        part_copy(turn).wait()
        here = pl.ds(pl.multiple_of(turn * 16, 16), 16)
        for c in range(3):
            fluid_at = part_send[c, here, :].astype(f32) + part_recv[c, here, :].astype(f32)
            old = motion[c, here, :]
            new = old + time_step * rate[here, :] * (fluid_at - old)
            updated[c, here, :] = new - time_step * gravity if c == 1 else new
        return carry

    stores = []

    def store(source, target):
        stores.append(pltpu.make_async_copy(source, target, store_sem.at[len(stores)]))
        stores[-1].start()

    for c in range(3):
        exchange_wait(3 + c)
        backward(c)
        store(planes_out.at[:, c], planes_any.at[:, c])
    lax.fori_loop(0, TILES // 16, sample, 0)
    lax.fori_loop(0, TILES // 16, update, 0)
    store(updated, updated_any)
    for index in range(6):
        sent_wait(index)
    for item in stores:
        item.wait()


def deliver_kernel(planes_any, updated_any, planes_out, updated_out, sem):
    copies = [
        pltpu.make_async_copy(planes_any.at[pl.ds(2 * i, 2)], planes_out.at[pl.ds(2 * i, 2)], sem.at[i])
        for i in range(4)
    ]
    copies.append(pltpu.make_async_copy(updated_any, updated_out, sem.at[4]))
    for item in copies:
        item.start()
    for item in copies:
        item.wait()


def on_device(
    cell_index,
    block_index,
    volume,
    response_rate,
    spanwise_position,
    particle_velocity,
    seen_velocity,
    fluid_velocity,
    eigen_basis,
    eigen_inverse,
    eigenvalues,
):
    tables = jnp.asarray(wave_tables())
    order = jnp.asarray(lane_order())
    particles = ((TILES, PT), f32)
    vectors = ((3, TILES, PT), f32)
    scratch = (
        ((TILES, PT), jnp.int32),
        particles,
        particles,
        particles,
        vectors,
        vectors,
        (tables.shape, bf16),
        (order.shape, bf16),
        ((NY * 6, 128), f32),
        ((NY, NY), f32),
        ((NY, NY), f32),
        ((2, TILES * WIDTH, 128), f32),
        ((4, MODES * 16, FOLD), bf16),
        ((TILES, 16, PT), f32),
        ((2, NY, NY), bf16),
        ((2, NY, NY), bf16),
        ((NY, 128), f32),
        ((3, NY, 256), f32),
        ((3, MODES, 16, KX), bf16),
        ((3, SLABS, 16, 128), bf16),
        ((3, SLABS, 16, 128), bf16),
        ((3, MODES, 16, KX), bf16),
        ((ROWS * MODES * 32, 128), f32),
        ((ROWS, 3, MODES * 32, 128), bf16),
        ((3, BLOCKS, 16, CB), bf16),
        vectors,
        ((3, TILES, PT), bf16),
        ((3, TILES, PT), bf16),
        vectors,
    )
    planes, updated = pl.pallas_call(
        flow_kernel,
        out_shape=(
            jax.ShapeDtypeStruct((ROWS, 3, MODES * 32, 128), bf16),
            jax.ShapeDtypeStruct((3, TILES, PT), f32),
        ),
        in_specs=[SMEM, VMEM, VMEM] + [ANY] * 11,
        out_specs=(ANY, ANY),
        scratch_shapes=[pltpu.VMEM(*item) for item in scratch]
        + [
            pltpu.SemaphoreType.DMA((11,)),
            pltpu.SemaphoreType.DMA((4,)),
            pltpu.SemaphoreType.DMA((6,)),
            pltpu.SemaphoreType.DMA((6,)),
            pltpu.SemaphoreType.DMA((6,)),
            pltpu.SemaphoreType.DMA((TILES // 16,)),
            pltpu.SemaphoreType.DMA((TILES // 16,)),
        ],
        compiler_params=pltpu.CompilerParams(
            collective_id=0, has_side_effects=True, vmem_limit_bytes=58 * 2**20
        ),
        name="flow",
    )(
        block_index,
        block_index.reshape(1, TILES),
        eigenvalues.reshape(1, NY),
        cell_index,
        spanwise_position,
        volume,
        response_rate,
        particle_velocity,
        seen_velocity,
        tables,
        order,
        fluid_velocity.reshape(NY * 6, 128),
        eigen_basis,
        eigen_inverse,
    )
    planes, updated = pl.pallas_call(
        deliver_kernel,
        out_shape=(
            jax.ShapeDtypeStruct(planes.shape, bf16),
            jax.ShapeDtypeStruct(updated.shape, f32),
        ),
        in_specs=[ANY, ANY],
        out_specs=(ANY, ANY),
        scratch_shapes=[pltpu.SemaphoreType.DMA((5,))],
        compiler_params=pltpu.CompilerParams(vmem_limit_bytes=58 * 2**20),
        name="deliver",
    )(planes, updated)
    planes = planes.reshape(ROWS, 3, MODES, 16, 2, 128)
    planes = jnp.transpose(planes, (0, 1, 2, 4, 3, 5)).reshape(ROWS, 3, MODES, 2, NX)
    return planes, updated


def solution(mesh):
    in_specs = (
        P(("px", "pz"), None),
        P(("px", "pz")),
        P(("px", "pz"), None),
        P(("px", "pz"), None),
        P(("px", "pz"), None),
        P(None, ("px", "pz"), None),
        P(None, ("px", "pz"), None),
        P(None, None, ("grp", "pz"), None, "px"),
        P(),
        P(),
        P(),
    )
    out_specs = (P(("px", "pz"), None, "grp", None, None), P(None, ("px", "pz"), None))
    return jax.shard_map(
        on_device, mesh=mesh, in_specs=in_specs, out_specs=out_specs, check_vma=False
    )
```

```python
import math

import jax
import jax.numpy as jnp
import ml_dtypes
import numpy as np
from jax import lax
from jax.experimental import pallas as pl
from jax.experimental.pallas import tpu as pltpu
from jax.sharding import PartitionSpec as P

NX = 2048
KX = 1024
NY = 512
CB = 256
PT = 512
TILES = 64
MODES = 8
ROWS = 8
STRIPS = 8
WIDTH = 3 * 2 * MODES
BLOCKS = ROWS * STRIPS
FOLD = NX // 4
KEPT = KX // 4
N_PX = 8
N_PZ = 8
SLABS = N_PX * N_PZ
TURN = 1.0 / (2.0 * math.pi)
COSINE = (
    1.0,
    -19.73920440673828,
    64.93911743164062,
    -85.45011138916016,
    60.16743087768555,
    -25.96688461303711,
    6.527706146240234,
)

time_step = 0.5
gravity = 0.8
viscosity = 0.0001

f32 = jnp.float32
bf16 = jnp.bfloat16
VMEM = pl.BlockSpec(memory_space=pltpu.VMEM)
SMEM = pl.BlockSpec(memory_space=pltpu.SMEM)
ANY = pl.BlockSpec(memory_space=pl.ANY)


def wave_tables():
    x = np.arange(FOLD, dtype=np.int64)[None, :, None]
    k = (
        4 * np.arange(KEPT, dtype=np.int64)[None, None, :]
        + np.arange(4, dtype=np.int64)[:, None, None]
        - KX // 2
    )
    angle = np.mod(k * x, NX) * (2.0 * math.pi / NX)
    table = np.stack([np.cos(angle), np.sin(angle)], axis=1) / math.sqrt(NX)
    return table.astype(np.float32).astype(ml_dtypes.bfloat16)


def lane_order():
    perm = np.zeros((128, 128), np.float32)
    lanes = np.arange(128)
    perm[4 * (lanes % 32) + lanes // 32, lanes] = 1.0
    return np.concatenate([perm, perm], axis=0).astype(ml_dtypes.bfloat16)


def cosine_turns(turns):
    part = turns - jnp.round(turns)
    square = part * part
    value = jnp.full_like(square, COSINE[-1])
    for term in COSINE[-2::-1]:
        value = value * square + term
    return value


def one_hot_cells(cell_row):
    cells = jnp.broadcast_to((cell_row & 127).astype(f32), (16, PT)).astype(bf16)
    lines = lax.broadcasted_iota(jnp.int32, (16, PT), 0).astype(f32).astype(bf16)
    one, zero = jnp.ones((16, PT), bf16), jnp.zeros((16, PT), bf16)
    return jnp.concatenate(
        [jnp.where(cells == lines + jnp.asarray(16 * i, bf16), one, zero) for i in range(8)],
        axis=0,
    )


def mode_turns(group):
    line = lax.broadcasted_iota(jnp.int32, (16, PT), 0)
    wave = (group * MODES + line % 8 + 1).astype(f32)
    shift = (line // 8).astype(f32) * 0.25
    return wave, shift


def swap_lanes(parts):
    return [
        jnp.concatenate([part[:, 32 * i : 32 * i + 32] for part in parts], axis=1)
        for i in range(4)
    ]


def dot(a, b):
    return lax.dot_general(a, b, (((1,), (0,)), ((), ())), preferred_element_type=f32)


def dot_t(a, b):
    return lax.dot_general(a, b, (((1,), (1,)), ((), ())), preferred_element_type=f32)


def block_fold(blocks_line):
    rows = lax.broadcasted_iota(jnp.int32, (128, 256), 0)
    lanes = lax.broadcasted_iota(jnp.int32, (128, 256), 1)
    q, s, r, y = rows // 32, (rows // 16) % 2, (rows // 8) % 2, rows % 8
    z = (lanes // TILES) % 2
    tile_block = jnp.broadcast_to(
        jnp.concatenate([blocks_line] * 4, axis=1), (128, 256)
    )
    strip = tile_block & 7
    turn = (q * (strip >> 1) + r - z + 4) & 3
    value = jnp.where(turn == 0, 1.0, jnp.where(turn == 2, -1.0, 0.0))
    here = ((tile_block >> 3) == y) & ((strip & 1) == s)
    return jnp.where(here, value, 0.0).astype(bf16)


def flow_kernel(
    block,
    block_line,
    eigenvalues,
    cell_any,
    place_any,
    volume_any,
    rate_any,
    motion_any,
    seen_any,
    tables_any,
    order_any,
    fluid_any,
    basis_any,
    inverse_any,
    planes_any,
    updated_any,
    cell,
    place,
    volume,
    rate,
    motion,
    seen,
    tables,
    order,
    fluid,
    basis,
    inverse,
    shares,
    folded,
    phases,
    split_basis,
    split_inverse,
    damping,
    ordered,
    forward_send,
    forward_recv,
    back_send,
    back_recv,
    planes,
    planes_out,
    blocks,
    part,
    part_send,
    part_recv,
    updated,
    load_sem,
    store_sem,
    own_sem,
    send_sem,
    recv_sem,
    part_send_sem,
    part_recv_sem,
):
    grp = lax.axis_index("grp")
    px = lax.axis_index("px")
    pz = lax.axis_index("pz")
    me = px * N_PZ + pz

    def peer(step):
        return lax.rem(px + step // N_PZ, N_PX), lax.rem(pz + lax.rem(step, N_PZ), N_PZ)

    sources = (cell_any, place_any, volume_any, rate_any, motion_any, seen_any)
    sources += (tables_any, order_any, fluid_any, basis_any, inverse_any)
    targets = (cell, place, volume, rate, motion, seen)
    targets += (tables, order, fluid, basis, inverse)
    loads = [
        pltpu.make_async_copy(source, target, load_sem.at[i])
        for i, (source, target) in enumerate(zip(sources, targets))
    ]
    for load in loads:
        load.start()

    barrier = pltpu.get_barrier_semaphore()

    def greet(step, carry):
        a, b = peer(step)
        pl.semaphore_signal(barrier, inc=1, device_id={"px": a, "pz": b})
        return carry

    pl.semaphore_signal(barrier, inc=1, device_id={"grp": 1 - grp})
    lax.fori_loop(1, SLABS, greet, 0)

    selection = block_fold(block_line[...])
    wave, shift = mode_turns(grp)
    for load in loads[:6]:
        load.wait()

    def deposit(turn, carry):
        first = pl.multiple_of(turn * 8, 8)
        here = pl.ds(first, 8)
        cells = cell[here, :]
        amount = volume[here, :]
        scale = amount * rate[here, :]
        angle = place[here, :] * TURN
        drags = [scale * (seen[c, here, :] - motion[c, here, :]) for c in range(3)]
        drags[1] = drags[1] - gravity * amount
        for i in range(8):
            phase = cosine_turns(
                wave * jnp.broadcast_to(angle[i : i + 1, :], (16, PT)) + shift
            )
            phases[first + i] = phase
            below = jnp.broadcast_to(cells[i : i + 1, :], (16, PT)) < 128
            lower, upper = [], []
            for c in range(3):
                payload = phase * jnp.broadcast_to(drags[c][i : i + 1, :], (16, PT))
                lower.append(jnp.where(below, payload, 0.0).astype(bf16))
                upper.append(jnp.where(below, 0.0, payload).astype(bf16))
            share = dot_t(
                jnp.concatenate(lower + upper, axis=0), one_hot_cells(cells[i : i + 1, :])
            )
            target = pl.ds(pl.multiple_of((first + i) * WIDTH, WIDTH), WIDTH)
            for h in range(2):
                shares[h, target, :] = share[WIDTH * h : WIDTH * h + WIDTH, :]
        return carry

    lax.fori_loop(0, TILES // 8, deposit, 0)

    def fold(c):
        for m in range(MODES):
            high, low = [], []
            for z in range(2):
                halves = [
                    shares[h, pl.ds(c * 16 + z * 8 + m, TILES, stride=WIDTH), :]
                    for h in range(2)
                ]
                value = jnp.concatenate(halves, axis=1)
                top = value.astype(bf16)
                high.append(top)
                low.append((value - top.astype(f32)).astype(bf16))
            sums = dot(selection, jnp.concatenate(high + low, axis=0))
            for q in range(4):
                for s in range(2):
                    first = q * 32 + s * 16
                    folded[q, m * 16 : m * 16 + 16, 256 * s : 256 * s + 256] = sums[
                        first : first + 16, :
                    ].astype(bf16)

    def forward(c):
        classes = []
        for q in range(4):
            even = dot(folded[q], tables[q, 0]).reshape(MODES, 2, ROWS, KEPT)
            odd = dot(folded[q], tables[q, 1]).reshape(MODES, 2, ROWS, KEPT)
            re = even[:, 0] + odd[:, 1]
            im = even[:, 1] - odd[:, 0]
            classes.append(
                jnp.concatenate([re, im], axis=1).reshape(MODES * 16, KEPT)
            )
        for h in range(2):
            chunks = swap_lanes([item[:, 128 * h : 128 * h + 128] for item in classes])
            for i in range(4):
                first = (4 * h + i) * 128
                forward_send[c, :, :, first : first + 128] = (
                    chunks[i].astype(bf16).reshape(MODES, 16, 128)
                )

    def forward_start(c):
        def send(step, carry):
            a, b = peer(step)
            pltpu.make_async_remote_copy(
                forward_send.at[c, b, :, pl.ds(pl.multiple_of(a * 128, 128), 128)],
                forward_recv.at[c, me],
                send_sem.at[c],
                recv_sem.at[c],
                device_id={"px": a, "pz": b},
            ).start()
            return carry

        pltpu.make_async_copy(
            forward_send.at[c, pz, :, pl.ds(pl.multiple_of(px * 128, 128), 128)],
            forward_recv.at[c, me],
            own_sem.at[c],
        ).start()
        lax.fori_loop(1, SLABS, send, 0)

    def back_start(c):
        def send(step, carry):
            a, b = peer(step)
            pltpu.make_async_remote_copy(
                back_send.at[c, a * N_PZ + b],
                back_recv.at[c, pz, :, pl.ds(pl.multiple_of(px * 128, 128), 128)],
                send_sem.at[3 + c],
                recv_sem.at[3 + c],
                device_id={"px": a, "pz": b},
            ).start()
            return carry

        pltpu.make_async_copy(
            back_send.at[c, me],
            back_recv.at[c, pz, :, pl.ds(pl.multiple_of(px * 128, 128), 128)],
            own_sem.at[3 + c],
        ).start()
        lax.fori_loop(1, SLABS, send, 0)

    def exchange_wait(index):
        blocks_in = forward_recv.at[0, pl.ds(0, SLABS - 1)]
        pltpu.make_async_remote_copy(
            blocks_in,
            blocks_in,
            send_sem.at[index],
            recv_sem.at[index],
            device_id={"px": px, "pz": pz},
        ).wait_recv()
        own = forward_recv.at[0, 0]
        pltpu.make_async_copy(own, own, own_sem.at[index]).wait()

    def sent_wait(index):
        blocks_out = forward_recv.at[0, pl.ds(0, SLABS - 1)]
        pltpu.make_async_remote_copy(
            blocks_out,
            blocks_out,
            send_sem.at[index],
            recv_sem.at[index],
            device_id={"px": px, "pz": pz},
        ).wait_send()

    fold(0)
    for load in loads[6:]:
        load.wait()
    forward(0)
    pl.semaphore_wait(barrier, SLABS)
    forward_start(0)
    for c in range(1, 3):
        fold(c)
        forward(c)
        forward_start(c)

    for matrix, split in ((basis, split_basis), (inverse, split_inverse)):
        high = matrix[...].astype(bf16)
        split[0] = high
        split[1] = (matrix[...] - high.astype(f32)).astype(bf16)
    lane = lax.broadcasted_iota(jnp.int32, (1, 128), 1)
    stream = px * 128 + 4 * (lane % 32) + lane // 32 - KX // 2
    stream = stream.astype(f32) * 0.5
    span = (grp * MODES + pz + 1).astype(f32)
    square = stream * stream + span * span
    column = jnp.transpose(jnp.broadcast_to(eigenvalues[...], (128, NY)))
    damping[...] = 1.0 / (1.0 + viscosity * (column + square))
    for c in range(3):
        for r in range(2):
            state = fluid[pl.ds(c * 2 + r, NY, stride=6), :]
            high = state.astype(bf16)
            low = (state - high.astype(f32)).astype(bf16)
            ordered[c, :, 128 * r : 128 * r + 128] = dot(
                jnp.concatenate([high, low], axis=1), order[...]
            )

    def apply(split, value):
        high = value.astype(bf16)
        low = (value - high.astype(f32)).astype(bf16)
        return dot(split[0], high) + (dot(split[0], low) + dot(split[1], high))

    for c in range(3):
        exchange_wait(c)
        forcing = forward_recv[c].astype(f32)
        force = jnp.concatenate(
            [forcing[:, 8 * r : 8 * r + 8, :].reshape(NY, 128) for r in range(2)], axis=1
        )
        modal = apply(split_inverse, ordered[c] + time_step * force)
        damp = damping[...]
        solved = apply(split_basis, modal * jnp.concatenate([damp, damp], axis=1))
        back_send[c] = jnp.concatenate(
            [solved[:, 128 * r : 128 * r + 128].reshape(SLABS, ROWS, 128) for r in range(2)],
            axis=1,
        ).astype(bf16)
        back_start(c)

    def backward(c):
        halves = []
        for h in range(2):
            parts = [
                back_recv[c, :, :, (4 * h + i) * 128 : (4 * h + i) * 128 + 128].reshape(
                    MODES * 16, 128
                )
                for i in range(4)
            ]
            halves.append(swap_lanes(parts))
        re, im = [], []
        for q in range(4):
            rows = jnp.concatenate([halves[0][q], halves[1][q]], axis=1)
            even = dot_t(rows, tables[q, 0]).reshape(MODES, 2, ROWS, FOLD)
            odd = dot_t(rows, tables[q, 1]).reshape(MODES, 2, ROWS, FOLD)
            re.append(even[:, 0] - odd[:, 1])
            im.append(odd[:, 0] + even[:, 1])
        sums = (re[0] + re[2], im[0] + im[2])
        lefts = (re[0] - re[2], im[0] - im[2])
        others = (re[1] + re[3], im[1] + im[3])
        rights = (im[3] - im[1], re[1] - re[3])
        results = (
            (sums[0] + others[0], sums[1] + others[1]),
            (lefts[0] + rights[0], lefts[1] + rights[1]),
            (sums[0] - others[0], sums[1] - others[1]),
            (lefts[0] - rights[0], lefts[1] - rights[1]),
        )
        for j in range(4):
            for r in range(2):
                for m in range(MODES):
                    for t in range(4):
                        planes[
                            pl.ds(m * 32 + (4 * j + t) * 2 + r, ROWS, stride=MODES * 32), :
                        ] = results[j][r][m, :, 128 * t : 128 * t + 128]

        def one_row(y, carry):
            first = pl.multiple_of(y * MODES * 32, MODES * 32)
            planes_out[y, c] = planes[pl.ds(first, MODES * 32), :].astype(bf16)
            for s in range(STRIPS):
                for h in range(2):
                    pair = [
                        planes[pl.ds(first + (2 * s + h) * 2 + r, MODES, stride=32), :]
                        for r in range(2)
                    ]
                    blocks[c, y * STRIPS + s, :, 128 * h : 128 * h + 128] = jnp.concatenate(
                        pair, axis=0
                    ).astype(bf16)
            return carry

        lax.fori_loop(0, ROWS, one_row, 0)

    def part_copy(turn):
        here = pl.ds(pl.multiple_of(turn * 16, 16), 16)
        return pltpu.make_async_remote_copy(
            part_send.at[:, here, :],
            part_recv.at[:, here, :],
            part_send_sem.at[turn],
            part_recv_sem.at[turn],
            device_id={"grp": 1 - grp},
        )

    def sample(turn, carry):
        for half in range(2):
            first = pl.multiple_of(turn * 16 + 8 * half, 8)
            here = pl.ds(first, 8)
            cells = cell[here, :]
            lines = [[], [], []]
            for i in range(8):
                own_block = block[first + i]
                rows = [blocks[c, own_block] for c in range(3)]
                rows = jnp.concatenate(
                    [item[:, :128] for item in rows] + [item[:, 128:] for item in rows], axis=0
                )
                both = dot(rows, one_hot_cells(cells[i : i + 1, :]))
                below = jnp.broadcast_to(cells[i : i + 1, :], (WIDTH, PT)) < 128
                picked = jnp.where(below, both[:WIDTH], both[WIDTH:])
                phase = phases[first + i]
                for c in range(3):
                    lines[c].append(
                        jnp.sum(picked[16 * c : 16 * c + 16, :] * phase, axis=0, keepdims=True)
                    )
            for c in range(3):
                part[c, here, :] = jnp.concatenate(lines[c], axis=0)
        here = pl.ds(pl.multiple_of(turn * 16, 16), 16)
        for c in range(3):
            part_send[c, here, :] = part[c, here, :].astype(bf16)
        part_copy(turn).start()
        return carry

    def update(turn, carry):
        part_copy(turn).wait()
        here = pl.ds(pl.multiple_of(turn * 16, 16), 16)
        for c in range(3):
            fluid_at = part_send[c, here, :].astype(f32) + part_recv[c, here, :].astype(f32)
            old = motion[c, here, :]
            new = old + time_step * rate[here, :] * (fluid_at - old)
            updated[c, here, :] = new - time_step * gravity if c == 1 else new
        return carry

    stores = []

    def store(source, target):
        stores.append(pltpu.make_async_copy(source, target, store_sem.at[len(stores)]))
        stores[-1].start()

    for c in range(3):
        exchange_wait(3 + c)
        backward(c)
        store(planes_out.at[:, c], planes_any.at[:, c])
    lax.fori_loop(0, TILES // 16, sample, 0)
    lax.fori_loop(0, TILES // 16, update, 0)
    store(updated, updated_any)
    for index in range(6):
        sent_wait(index)
    for item in stores:
        item.wait()


def deliver_kernel(planes_any, updated_any, planes_out, updated_out, planes, updated, load_sem, store_sem):
    pairs = [
        (planes_any.at[pl.ds(2 * i, 2)], planes.at[pl.ds(2 * i, 2)], planes_out.at[pl.ds(2 * i, 2)])
        for i in range(4)
    ]
    pairs.append((updated_any, updated, updated_out))
    loads = [pltpu.make_async_copy(a, b, load_sem.at[i]) for i, (a, b, c) in enumerate(pairs)]
    stores = [pltpu.make_async_copy(b, c, store_sem.at[i]) for i, (a, b, c) in enumerate(pairs)]
    for load in loads:
        load.start()
    for load, store in zip(loads, stores):
        load.wait()
        store.start()
    for store in stores:
        store.wait()


def on_device(
    cell_index,
    block_index,
    volume,
    response_rate,
    spanwise_position,
    particle_velocity,
    seen_velocity,
    fluid_velocity,
    eigen_basis,
    eigen_inverse,
    eigenvalues,
):
    tables = jnp.asarray(wave_tables())
    order = jnp.asarray(lane_order())
    particles = ((TILES, PT), f32)
    vectors = ((3, TILES, PT), f32)
    scratch = (
        ((TILES, PT), jnp.int32),
        particles,
        particles,
        particles,
        vectors,
        vectors,
        (tables.shape, bf16),
        (order.shape, bf16),
        ((NY * 6, 128), f32),
        ((NY, NY), f32),
        ((NY, NY), f32),
        ((2, TILES * WIDTH, 128), f32),
        ((4, MODES * 16, FOLD), bf16),
        ((TILES, 16, PT), f32),
        ((2, NY, NY), bf16),
        ((2, NY, NY), bf16),
        ((NY, 128), f32),
        ((3, NY, 256), f32),
        ((3, MODES, 16, KX), bf16),
        ((3, SLABS, 16, 128), bf16),
        ((3, SLABS, 16, 128), bf16),
        ((3, MODES, 16, KX), bf16),
        ((ROWS * MODES * 32, 128), f32),
        ((ROWS, 3, MODES * 32, 128), bf16),
        ((3, BLOCKS, 16, CB), bf16),
        vectors,
        ((3, TILES, PT), bf16),
        ((3, TILES, PT), bf16),
        vectors,
    )
    planes, updated = pl.pallas_call(
        flow_kernel,
        out_shape=(
            jax.ShapeDtypeStruct((ROWS, 3, MODES * 32, 128), bf16),
            jax.ShapeDtypeStruct((3, TILES, PT), f32),
        ),
        in_specs=[SMEM, VMEM, VMEM] + [ANY] * 11,
        out_specs=(ANY, ANY),
        scratch_shapes=[pltpu.VMEM(*item) for item in scratch]
        + [
            pltpu.SemaphoreType.DMA((11,)),
            pltpu.SemaphoreType.DMA((4,)),
            pltpu.SemaphoreType.DMA((6,)),
            pltpu.SemaphoreType.DMA((6,)),
            pltpu.SemaphoreType.DMA((6,)),
            pltpu.SemaphoreType.DMA((TILES // 16,)),
            pltpu.SemaphoreType.DMA((TILES // 16,)),
        ],
        compiler_params=pltpu.CompilerParams(
            collective_id=0, has_side_effects=True, vmem_limit_bytes=58 * 2**20
        ),
        name="flow",
    )(
        block_index,
        block_index.reshape(1, TILES),
        eigenvalues.reshape(1, NY),
        cell_index,
        spanwise_position,
        volume,
        response_rate,
        particle_velocity,
        seen_velocity,
        tables,
        order,
        fluid_velocity.reshape(NY * 6, 128),
        eigen_basis,
        eigen_inverse,
    )
    planes, updated = pl.pallas_call(
        deliver_kernel,
        out_shape=(
            jax.ShapeDtypeStruct(planes.shape, bf16),
            jax.ShapeDtypeStruct(updated.shape, f32),
        ),
        in_specs=[ANY, ANY],
        out_specs=(ANY, ANY),
        scratch_shapes=[
            pltpu.VMEM(planes.shape, bf16),
            pltpu.VMEM(updated.shape, f32),
            pltpu.SemaphoreType.DMA((5,)),
            pltpu.SemaphoreType.DMA((5,)),
        ],
        compiler_params=pltpu.CompilerParams(vmem_limit_bytes=58 * 2**20),
        name="deliver",
    )(planes, updated)
    planes = planes.reshape(ROWS, 3, MODES, 16, 2, 128)
    planes = jnp.transpose(planes, (0, 1, 2, 4, 3, 5)).reshape(ROWS, 3, MODES, 2, NX)
    return planes, updated


def solution(mesh):
    in_specs = (
        P(("px", "pz"), None),
        P(("px", "pz")),
        P(("px", "pz"), None),
        P(("px", "pz"), None),
        P(("px", "pz"), None),
        P(None, ("px", "pz"), None),
        P(None, ("px", "pz"), None),
        P(None, None, ("grp", "pz"), None, "px"),
        P(),
        P(),
        P(),
    )
    out_specs = (P(("px", "pz"), None, "grp", None, None), P(None, ("px", "pz"), None))
    return jax.shard_map(
        on_device, mesh=mesh, in_specs=in_specs, out_specs=out_specs, check_vma=False
    )
```

```python
import math

import jax
import jax.numpy as jnp
import ml_dtypes
import numpy as np
from jax import lax
from jax.experimental import pallas as pl
from jax.experimental.pallas import tpu as pltpu
from jax.sharding import PartitionSpec as P

NX = 2048
KX = 1024
NY = 512
CB = 256
PT = 512
TILES = 64
MODES = 8
ROWS = 8
STRIPS = 8
WIDTH = 3 * 2 * MODES
BLOCKS = ROWS * STRIPS
FOLD = NX // 4
KEPT = KX // 4
PASSES = ((0, 1), (2,))
N_PX = 8
N_PZ = 8
SLABS = N_PX * N_PZ
TURN = 1.0 / (2.0 * math.pi)
COSINE = (
    1.0,
    -19.73920440673828,
    64.93911743164062,
    -85.45011138916016,
    60.16743087768555,
    -25.96688461303711,
    6.527706146240234,
)

time_step = 0.5
gravity = 0.8
viscosity = 0.0001

f32 = jnp.float32
bf16 = jnp.bfloat16
VMEM = pl.BlockSpec(memory_space=pltpu.VMEM)
HBM = pl.BlockSpec(memory_space=pltpu.HBM)


def wave_tables():
    x = np.arange(FOLD, dtype=np.int64)[None, :, None]
    k = (
        4 * np.arange(KEPT, dtype=np.int64)[None, None, :]
        + np.arange(4, dtype=np.int64)[:, None, None]
        - KX // 2
    )
    angle = np.mod(k * x, NX) * (2.0 * math.pi / NX)
    table = np.stack([np.cos(angle), np.sin(angle)], axis=1) / math.sqrt(NX)
    return table.astype(np.float32).astype(ml_dtypes.bfloat16)


def lane_order():
    perm = np.zeros((128, 128), np.float32)
    lanes = np.arange(128)
    perm[4 * (lanes % 32) + lanes // 32, lanes] = 1.0
    return np.concatenate([perm, perm], axis=0).astype(ml_dtypes.bfloat16)


def cosine_turns(turns):
    part = turns - jnp.round(turns)
    square = part * part
    value = jnp.full_like(square, COSINE[-1])
    for term in COSINE[-2::-1]:
        value = value * square + term
    return value


def one_hot_cells(cell_row):
    cells = jnp.broadcast_to((cell_row & 127).astype(f32), (16, PT)).astype(bf16)
    lines = lax.broadcasted_iota(jnp.int32, (16, PT), 0).astype(f32).astype(bf16)
    one, zero = jnp.ones((16, PT), bf16), jnp.zeros((16, PT), bf16)
    return jnp.concatenate(
        [jnp.where(cells == lines + jnp.asarray(16 * i, bf16), one, zero) for i in range(8)],
        axis=0,
    )


def mode_turns(group):
    line = lax.broadcasted_iota(jnp.int32, (16, PT), 0)
    wave = (group * MODES + line % 8 + 1).astype(f32)
    shift = (line // 8).astype(f32) * 0.25
    return wave, shift


def swap_lanes(parts):
    return [
        jnp.concatenate([part[:, 32 * i : 32 * i + 32] for part in parts], axis=1)
        for i in range(4)
    ]


def dot(a, b):
    return lax.dot_general(a, b, (((1,), (0,)), ((), ())), preferred_element_type=f32)


def dot_t(a, b):
    return lax.dot_general(a, b, (((1,), (1,)), ((), ())), preferred_element_type=f32)


def block_fold(blocks_line):
    rows = lax.broadcasted_iota(jnp.int32, (128, 256), 0)
    lanes = lax.broadcasted_iota(jnp.int32, (128, 256), 1)
    q, s, r, y = rows // 32, (rows // 16) % 2, (rows // 8) % 2, rows % 8
    z = (lanes // TILES) % 2
    tile_block = jnp.broadcast_to(
        jnp.concatenate([blocks_line] * 4, axis=1), (128, 256)
    )
    strip = tile_block & 7
    turn = (q * (strip >> 1) + r - z + 4) & 3
    value = jnp.where(turn == 0, 1.0, jnp.where(turn == 2, -1.0, 0.0))
    here = ((tile_block >> 3) == y) & ((strip & 1) == s)
    return jnp.where(here, value, 0.0).astype(bf16)


def flow_kernel(
    block_any,
    block_line_any,
    eigenvalues_any,
    cell_any,
    place_any,
    volume_any,
    rate_any,
    motion_any,
    seen_any,
    tables_any,
    order_any,
    fluid_any,
    basis_any,
    inverse_any,
    planes_out,
    updated,
    block,
    block_line,
    eigenvalues,
    cell,
    place,
    volume,
    rate,
    motion,
    seen,
    tables,
    order,
    fluid,
    basis,
    inverse,
    shares,
    folded,
    phases,
    split_basis,
    split_inverse,
    damping,
    ordered,
    forward_send,
    forward_recv,
    back_send,
    back_recv,
    planes,
    blocks,
    part,
    part_send,
    part_recv,
    load_sem,
    own_sem,
    send_sem,
    recv_sem,
    part_send_sem,
    part_recv_sem,
):
    grp = lax.axis_index("grp")
    px = lax.axis_index("px")
    pz = lax.axis_index("pz")
    me = px * N_PZ + pz

    def peer(step):
        return lax.rem(px + step // N_PZ, N_PX), lax.rem(pz + lax.rem(step, N_PZ), N_PZ)

    sources = (cell_any, place_any, volume_any, rate_any, motion_any, seen_any)
    sources += (block_line_any, block_any, eigenvalues_any, tables_any, order_any, fluid_any, basis_any, inverse_any)
    targets = (cell, place, volume, rate, motion, seen)
    targets += (block_line, block, eigenvalues, tables, order, fluid, basis, inverse)
    loads = [
        pltpu.make_async_copy(source, target, load_sem.at[i])
        for i, (source, target) in enumerate(zip(sources, targets))
    ]
    for load in loads:
        load.start()

    barrier = pltpu.get_barrier_semaphore()

    def greet(step, carry):
        a, b = peer(step)
        pl.semaphore_signal(barrier, inc=1, device_id={"px": a, "pz": b})
        return carry

    pl.semaphore_signal(barrier, inc=1, device_id={"grp": 1 - grp})
    lax.fori_loop(1, SLABS, greet, 0)

    wave, shift = mode_turns(grp)
    for load in loads[:7]:
        load.wait()
    selection = block_fold(block_line[...])

    def deposit(turn, carry):
        first = pl.multiple_of(turn * 8, 8)
        here = pl.ds(first, 8)
        cells = cell[here, :]
        amount = volume[here, :]
        scale = amount * rate[here, :]
        angle = place[here, :] * TURN
        drags = [scale * (seen[c, here, :] - motion[c, here, :]) for c in range(3)]
        drags[1] = drags[1] - gravity * amount
        for i in range(8):
            phase = cosine_turns(
                wave * jnp.broadcast_to(angle[i : i + 1, :], (16, PT)) + shift
            )
            phases[first + i] = phase
            below = jnp.broadcast_to(cells[i : i + 1, :], (16, PT)) < 128
            lower, upper = [], []
            for c in range(3):
                payload = phase * jnp.broadcast_to(drags[c][i : i + 1, :], (16, PT))
                lower.append(jnp.where(below, payload, 0.0).astype(bf16))
                upper.append(jnp.where(below, 0.0, payload).astype(bf16))
            share = dot_t(
                jnp.concatenate(lower + upper, axis=0), one_hot_cells(cells[i : i + 1, :])
            )
            target = pl.ds(pl.multiple_of((first + i) * WIDTH, WIDTH), WIDTH)
            for h in range(2):
                shares[h, target, :] = share[WIDTH * h : WIDTH * h + WIDTH, :]
        return carry

    lax.fori_loop(0, TILES // 8, deposit, 0)

    def fold(c):
        for m in range(MODES):
            high, low = [], []
            for z in range(2):
                halves = [
                    shares[h, pl.ds(c * 16 + z * 8 + m, TILES, stride=WIDTH), :]
                    for h in range(2)
                ]
                value = jnp.concatenate(halves, axis=1)
                top = value.astype(bf16)
                high.append(top)
                low.append((value - top.astype(f32)).astype(bf16))
            sums = dot(selection, jnp.concatenate(high + low, axis=0))
            for q in range(4):
                for s in range(2):
                    first = q * 32 + s * 16
                    folded[q, m * 16 : m * 16 + 16, 256 * s : 256 * s + 256] = sums[
                        first : first + 16, :
                    ].astype(bf16)

    def forward(c):
        classes = []
        for q in range(4):
            even = dot(folded[q], tables[q, 0]).reshape(MODES, 2, ROWS, KEPT)
            odd = dot(folded[q], tables[q, 1]).reshape(MODES, 2, ROWS, KEPT)
            re = even[:, 0] + odd[:, 1]
            im = even[:, 1] - odd[:, 0]
            classes.append(
                jnp.concatenate([re, im], axis=1).reshape(MODES * 16, KEPT)
            )
        for h in range(2):
            chunks = swap_lanes([item[:, 128 * h : 128 * h + 128] for item in classes])
            for i in range(4):
                first = (4 * h + i) * 128
                forward_send[c, :, :, first : first + 128] = (
                    chunks[i].astype(bf16).reshape(MODES, 16, 128)
                )

    def forward_start(c):
        def send(step, carry):
            a, b = peer(step)
            pltpu.make_async_remote_copy(
                forward_send.at[c, b, :, pl.ds(pl.multiple_of(a * 128, 128), 128)],
                forward_recv.at[c, me],
                send_sem.at[c],
                recv_sem.at[c],
                device_id={"px": a, "pz": b},
            ).start()
            return carry

        pltpu.make_async_copy(
            forward_send.at[c, pz, :, pl.ds(pl.multiple_of(px * 128, 128), 128)],
            forward_recv.at[c, me],
            own_sem.at[c],
        ).start()
        lax.fori_loop(1, SLABS, send, 0)

    def back_start(c):
        def send(step, carry):
            a, b = peer(step)
            pltpu.make_async_remote_copy(
                back_send.at[c, a * N_PZ + b],
                back_recv.at[c, pz, :, pl.ds(pl.multiple_of(px * 128, 128), 128)],
                send_sem.at[3 + c],
                recv_sem.at[3 + c],
                device_id={"px": a, "pz": b},
            ).start()
            return carry

        pltpu.make_async_copy(
            back_send.at[c, me],
            back_recv.at[c, pz, :, pl.ds(pl.multiple_of(px * 128, 128), 128)],
            own_sem.at[3 + c],
        ).start()
        lax.fori_loop(1, SLABS, send, 0)

    def exchange_wait(index):
        blocks_in = forward_recv.at[0, pl.ds(0, SLABS - 1)]
        pltpu.make_async_remote_copy(
            blocks_in,
            blocks_in,
            send_sem.at[index],
            recv_sem.at[index],
            device_id={"px": px, "pz": pz},
        ).wait_recv()
        own = forward_recv.at[0, 0]
        pltpu.make_async_copy(own, own, own_sem.at[index]).wait()

    def sent_wait(index):
        blocks_out = forward_recv.at[0, pl.ds(0, SLABS - 1)]
        pltpu.make_async_remote_copy(
            blocks_out,
            blocks_out,
            send_sem.at[index],
            recv_sem.at[index],
            device_id={"px": px, "pz": pz},
        ).wait_send()

    fold(0)
    for load in loads[7:]:
        load.wait()
    forward(0)
    pl.semaphore_wait(barrier, SLABS)
    forward_start(0)
    for c in range(1, 3):
        fold(c)
        forward(c)
        forward_start(c)

    for matrix, split in ((basis, split_basis), (inverse, split_inverse)):
        high = matrix[...].astype(bf16)
        split[0] = high
        split[1] = (matrix[...] - high.astype(f32)).astype(bf16)
    lane = lax.broadcasted_iota(jnp.int32, (1, 128), 1)
    stream = px * 128 + 4 * (lane % 32) + lane // 32 - KX // 2
    stream = stream.astype(f32) * 0.5
    span = (grp * MODES + pz + 1).astype(f32)
    square = stream * stream + span * span
    column = jnp.transpose(jnp.broadcast_to(eigenvalues[...], (128, NY)))
    damping[...] = 1.0 / (1.0 + viscosity * (column + square))
    for c in range(3):
        for r in range(2):
            state = fluid[pl.ds(c * 2 + r, NY, stride=6), :]
            high = state.astype(bf16)
            low = (state - high.astype(f32)).astype(bf16)
            ordered[c, :, 128 * r : 128 * r + 128] = dot(
                jnp.concatenate([high, low], axis=1), order[...]
            )

    def apply(split, value):
        high = value.astype(bf16)
        low = (value - high.astype(f32)).astype(bf16)
        return dot(split[0], high) + (dot(split[0], low) + dot(split[1], high))

    for c in range(3):
        exchange_wait(c)
        forcing = forward_recv[c].astype(f32)
        force = jnp.concatenate(
            [forcing[:, 8 * r : 8 * r + 8, :].reshape(NY, 128) for r in range(2)], axis=1
        )
        modal = apply(split_inverse, ordered[c] + time_step * force)
        damp = damping[...]
        solved = apply(split_basis, modal * jnp.concatenate([damp, damp], axis=1))
        back_send[c] = jnp.concatenate(
            [solved[:, 128 * r : 128 * r + 128].reshape(SLABS, ROWS, 128) for r in range(2)],
            axis=1,
        ).astype(bf16)
        back_start(c)

    def backward(c):
        halves = []
        for h in range(2):
            parts = [
                back_recv[c, :, :, (4 * h + i) * 128 : (4 * h + i) * 128 + 128].reshape(
                    MODES * 16, 128
                )
                for i in range(4)
            ]
            halves.append(swap_lanes(parts))
        re, im = [], []
        for q in range(4):
            rows = jnp.concatenate([halves[0][q], halves[1][q]], axis=1)
            even = dot_t(rows, tables[q, 0]).reshape(MODES, 2, ROWS, FOLD)
            odd = dot_t(rows, tables[q, 1]).reshape(MODES, 2, ROWS, FOLD)
            re.append(even[:, 0] - odd[:, 1])
            im.append(odd[:, 0] + even[:, 1])
        sums = (re[0] + re[2], im[0] + im[2])
        lefts = (re[0] - re[2], im[0] - im[2])
        others = (re[1] + re[3], im[1] + im[3])
        rights = (im[3] - im[1], re[1] - re[3])
        results = (
            (sums[0] + others[0], sums[1] + others[1]),
            (lefts[0] + rights[0], lefts[1] + rights[1]),
            (sums[0] - others[0], sums[1] - others[1]),
            (lefts[0] - rights[0], lefts[1] - rights[1]),
        )
        for j in range(4):
            for r in range(2):
                for m in range(MODES):
                    for t in range(4):
                        planes[
                            pl.ds(m * 32 + (4 * j + t) * 2 + r, ROWS, stride=MODES * 32), :
                        ] = results[j][r][m, :, 128 * t : 128 * t + 128]

        def one_row(y, carry):
            first = pl.multiple_of(y * MODES * 32, MODES * 32)
            planes_out[y, c] = planes[pl.ds(first, MODES * 32), :].astype(bf16)
            for s in range(STRIPS):
                for h in range(2):
                    pair = [
                        planes[pl.ds(first + (2 * s + h) * 2 + r, MODES, stride=32), :]
                        for r in range(2)
                    ]
                    blocks[c, y * STRIPS + s, :, 128 * h : 128 * h + 128] = jnp.concatenate(
                        pair, axis=0
                    ).astype(bf16)
            return carry

        lax.fori_loop(0, ROWS, one_row, 0)

    def part_copy(group, turn):
        here = (pl.ds(group[0], len(group)), pl.ds(pl.multiple_of(turn * 16, 16), 16))
        return pltpu.make_async_remote_copy(
            part_send.at[here],
            part_recv.at[here],
            part_send_sem.at[group[0], turn],
            part_recv_sem.at[group[0], turn],
            device_id={"grp": 1 - grp},
        )

    def sample(group):
        def sixteen_tiles(turn, carry):
            for half in range(2):
                first = pl.multiple_of(turn * 16 + 8 * half, 8)
                here = pl.ds(first, 8)
                cells = cell[here, :]
                lines = [[] for c in group]
                width = 16 * len(group)
                for i in range(8):
                    own_block = block[first + i]
                    rows = [blocks[c, own_block] for c in group]
                    rows = jnp.concatenate(
                        [item[:, :128] for item in rows] + [item[:, 128:] for item in rows], axis=0
                    )
                    both = dot(rows, one_hot_cells(cells[i : i + 1, :]))
                    below = jnp.broadcast_to(cells[i : i + 1, :], (width, PT)) < 128
                    picked = jnp.where(below, both[:width], both[width:])
                    phase = phases[first + i]
                    for n in range(len(group)):
                        lines[n].append(
                            jnp.sum(
                                picked[16 * n : 16 * n + 16, :] * phase, axis=0, keepdims=True
                            )
                        )
                for n, c in enumerate(group):
                    part[c, here, :] = jnp.concatenate(lines[n], axis=0)
            here = pl.ds(pl.multiple_of(turn * 16, 16), 16)
            for c in group:
                part_send[c, here, :] = part[c, here, :].astype(bf16)
            part_copy(group, turn).start()
            return carry

        lax.fori_loop(0, TILES // 16, sixteen_tiles, 0)

    def update(group):
        def sixteen_tiles(turn, carry):
            part_copy(group, turn).wait()
            here = pl.ds(pl.multiple_of(turn * 16, 16), 16)
            for c in group:
                fluid_at = part_send[c, here, :].astype(f32) + part_recv[c, here, :].astype(f32)
                old = motion[c, here, :]
                new = old + time_step * rate[here, :] * (fluid_at - old)
                updated[c, here, :] = new - time_step * gravity if c == 1 else new
            return carry

        lax.fori_loop(0, TILES // 16, sixteen_tiles, 0)

    for group in PASSES:
        for c in group:
            exchange_wait(3 + c)
            backward(c)
        sample(group)
    for group in PASSES:
        update(group)
    for index in range(6):
        sent_wait(index)


def deliver_kernel(planes, updated, planes_out, updated_out, sem):
    stores = [
        pltpu.make_async_copy(
            planes.at[pl.ds(2 * i, 2)], planes_out.at[pl.ds(2 * i, 2)], sem.at[i]
        )
        for i in range(4)
    ]
    stores.append(pltpu.make_async_copy(updated, updated_out, sem.at[4]))
    for store in stores:
        store.start()
    for store in stores:
        store.wait()


def on_device(
    cell_index,
    block_index,
    volume,
    response_rate,
    spanwise_position,
    particle_velocity,
    seen_velocity,
    fluid_velocity,
    eigen_basis,
    eigen_inverse,
    eigenvalues,
):
    tables = jnp.asarray(wave_tables())
    order = jnp.asarray(lane_order())
    particles = ((TILES, PT), f32)
    vectors = ((3, TILES, PT), f32)
    scratch = (
        ((1, TILES), jnp.int32),
        ((1, NY), f32),
        ((TILES, PT), jnp.int32),
        particles,
        particles,
        particles,
        vectors,
        vectors,
        (tables.shape, bf16),
        (order.shape, bf16),
        ((NY * 6, 128), f32),
        ((NY, NY), f32),
        ((NY, NY), f32),
        ((2, TILES * WIDTH, 128), f32),
        ((4, MODES * 16, FOLD), bf16),
        ((TILES, 16, PT), f32),
        ((2, NY, NY), bf16),
        ((2, NY, NY), bf16),
        ((NY, 128), f32),
        ((3, NY, 256), f32),
        ((3, MODES, 16, KX), bf16),
        ((3, SLABS, 16, 128), bf16),
        ((3, SLABS, 16, 128), bf16),
        ((3, MODES, 16, KX), bf16),
        ((ROWS * MODES * 32, 128), f32),
        ((3, BLOCKS, 16, CB), bf16),
        vectors,
        ((3, TILES, PT), bf16),
        ((3, TILES, PT), bf16),
    )
    planes, updated = pl.pallas_call(
        flow_kernel,
        out_shape=(
            jax.ShapeDtypeStruct((ROWS, 3, MODES * 32, 128), bf16),
            jax.ShapeDtypeStruct((3, TILES, PT), f32),
        ),
        in_specs=[HBM] * 14,
        out_specs=(VMEM, VMEM),
        scratch_shapes=[pltpu.SMEM((TILES,), jnp.int32)]
        + [pltpu.VMEM(*item) for item in scratch]
        + [
            pltpu.SemaphoreType.DMA((14,)),
            pltpu.SemaphoreType.DMA((6,)),
            pltpu.SemaphoreType.DMA((6,)),
            pltpu.SemaphoreType.DMA((6,)),
            pltpu.SemaphoreType.DMA((3, TILES // 16)),
            pltpu.SemaphoreType.DMA((3, TILES // 16)),
        ],
        compiler_params=pltpu.CompilerParams(
            collective_id=0, has_side_effects=True, vmem_limit_bytes=36 * 2**20
        ),
        name="flow",
    )(*(
        pltpu.with_memory_space_constraint(item, pltpu.HBM)
        for item in (
        block_index,
        block_index.reshape(1, TILES),
        eigenvalues.reshape(1, NY),
        cell_index,
        spanwise_position,
        volume,
        response_rate,
        particle_velocity,
        seen_velocity,
        tables,
        order,
        fluid_velocity.reshape(NY * 6, 128),
        eigen_basis,
        eigen_inverse,
            )
    ))
    planes, updated = pl.pallas_call(
        deliver_kernel,
        out_shape=(
            jax.ShapeDtypeStruct(planes.shape, bf16),
            jax.ShapeDtypeStruct((3, TILES, PT), f32),
        ),
        in_specs=[VMEM, VMEM],
        out_specs=(HBM, HBM),
        scratch_shapes=[pltpu.SemaphoreType.DMA((5,))],
        compiler_params=pltpu.CompilerParams(vmem_limit_bytes=8 * 2**20),
        name="deliver",
    )(planes, updated)
    planes = planes.reshape(ROWS, 3, MODES, 16, 2, 128)
    planes = jnp.transpose(planes, (0, 1, 2, 4, 3, 5)).reshape(ROWS, 3, MODES, 2, NX)
    return planes, updated


def solution(mesh):
    in_specs = (
        P(("px", "pz"), None),
        P(("px", "pz")),
        P(("px", "pz"), None),
        P(("px", "pz"), None),
        P(("px", "pz"), None),
        P(None, ("px", "pz"), None),
        P(None, ("px", "pz"), None),
        P(None, None, ("grp", "pz"), None, "px"),
        P(),
        P(),
        P(),
    )
    out_specs = (P(("px", "pz"), None, "grp", None, None), P(None, ("px", "pz"), None))
    return jax.shard_map(
        on_device, mesh=mesh, in_specs=in_specs, out_specs=out_specs, check_vma=False
    )
```

```python
import math

import jax
import jax.numpy as jnp
import ml_dtypes
import numpy as np
from jax import lax
from jax.experimental import pallas as pl
from jax.experimental.pallas import tpu as pltpu
from jax.sharding import PartitionSpec as P

NX = 2048
KX = 1024
NY = 512
CB = 256
PT = 512
TILES = 64
MODES = 8
ROWS = 8
STRIPS = 8
WIDTH = 3 * 2 * MODES
BLOCKS = ROWS * STRIPS
FOLD = NX // 4
KEPT = KX // 4
PASSES = ((0, 1), (2,))
N_PX = 8
N_PZ = 8
SLABS = N_PX * N_PZ
TURN = 1.0 / (2.0 * math.pi)
COSINE = (
    1.0,
    -19.73920440673828,
    64.93911743164062,
    -85.45011138916016,
    60.16743087768555,
    -25.96688461303711,
    6.527706146240234,
)

time_step = 0.5
gravity = 0.8
viscosity = 0.0001

f32 = jnp.float32
bf16 = jnp.bfloat16
VMEM = pl.BlockSpec(memory_space=pltpu.VMEM)
HBM = pl.BlockSpec(memory_space=pltpu.HBM)


def wave_tables():
    x = np.arange(FOLD, dtype=np.int64)[None, :, None]
    k = (
        4 * np.arange(KEPT, dtype=np.int64)[None, None, :]
        + np.arange(4, dtype=np.int64)[:, None, None]
        - KX // 2
    )
    angle = np.mod(k * x, NX) * (2.0 * math.pi / NX)
    table = np.stack([np.cos(angle), np.sin(angle)], axis=1) / math.sqrt(NX)
    return table.astype(np.float32).astype(ml_dtypes.bfloat16)


def lane_order():
    perm = np.zeros((128, 128), np.float32)
    lanes = np.arange(128)
    perm[4 * (lanes % 32) + lanes // 32, lanes] = 1.0
    return np.concatenate([perm, perm], axis=0).astype(ml_dtypes.bfloat16)


def cosine_turns(turns):
    part = turns - jnp.round(turns)
    square = part * part
    value = jnp.full_like(square, COSINE[-1])
    for term in COSINE[-2::-1]:
        value = value * square + term
    return value


def one_hot_cells(cell_row):
    cells = jnp.broadcast_to((cell_row & 127).astype(f32), (16, PT)).astype(bf16)
    lines = lax.broadcasted_iota(jnp.int32, (16, PT), 0).astype(f32).astype(bf16)
    one, zero = jnp.ones((16, PT), bf16), jnp.zeros((16, PT), bf16)
    return jnp.concatenate(
        [jnp.where(cells == lines + jnp.asarray(16 * i, bf16), one, zero) for i in range(8)],
        axis=0,
    )


def mode_turns(group):
    line = lax.broadcasted_iota(jnp.int32, (16, PT), 0)
    wave = (group * MODES + line % 8 + 1).astype(f32)
    shift = (line // 8).astype(f32) * 0.25
    return wave, shift


def swap_lanes(parts):
    return [
        jnp.concatenate([part[:, 32 * i : 32 * i + 32] for part in parts], axis=1)
        for i in range(4)
    ]


def dot(a, b):
    return lax.dot_general(a, b, (((1,), (0,)), ((), ())), preferred_element_type=f32)


def dot_t(a, b):
    return lax.dot_general(a, b, (((1,), (1,)), ((), ())), preferred_element_type=f32)


def block_fold(blocks_line):
    rows = lax.broadcasted_iota(jnp.int32, (128, 256), 0)
    lanes = lax.broadcasted_iota(jnp.int32, (128, 256), 1)
    q, s, r, y = rows // 32, (rows // 16) % 2, (rows // 8) % 2, rows % 8
    z = (lanes // TILES) % 2
    tile_block = jnp.broadcast_to(
        jnp.concatenate([blocks_line] * 4, axis=1), (128, 256)
    )
    strip = tile_block & 7
    turn = (q * (strip >> 1) + r - z + 4) & 3
    value = jnp.where(turn == 0, 1.0, jnp.where(turn == 2, -1.0, 0.0))
    here = ((tile_block >> 3) == y) & ((strip & 1) == s)
    return jnp.where(here, value, 0.0).astype(bf16)


def flow_kernel(
    block_any,
    block_line_any,
    eigenvalues_any,
    tables_back_any,
    cell_any,
    place_any,
    volume_any,
    rate_any,
    motion_any,
    seen_any,
    tables_any,
    order_any,
    fluid_any,
    basis_any,
    inverse_any,
    planes_out,
    updated,
    block,
    block_line,
    eigenvalues,
    tables_back,
    cell,
    place,
    volume,
    rate,
    motion,
    seen,
    tables,
    order,
    fluid,
    basis,
    inverse,
    shares,
    folded,
    phases,
    split_basis,
    split_inverse,
    damping,
    ordered,
    forward_send,
    forward_recv,
    back_send,
    back_recv,
    planes,
    blocks,
    part,
    part_send,
    part_recv,
    load_sem,
    own_sem,
    send_sem,
    recv_sem,
    part_send_sem,
    part_recv_sem,
):
    grp = lax.axis_index("grp")
    px = lax.axis_index("px")
    pz = lax.axis_index("pz")
    me = px * N_PZ + pz

    def peer(step):
        return lax.rem(px + step // N_PZ, N_PX), lax.rem(pz + lax.rem(step, N_PZ), N_PZ)

    sources = (cell_any, place_any, volume_any, rate_any, motion_any, seen_any)
    sources += (block_line_any, block_any, eigenvalues_any, tables_back_any, tables_any, order_any, fluid_any, basis_any, inverse_any)
    targets = (cell, place, volume, rate, motion, seen)
    targets += (block_line, block, eigenvalues, tables_back, tables, order, fluid, basis, inverse)
    loads = [
        pltpu.make_async_copy(source, target, load_sem.at[i])
        for i, (source, target) in enumerate(zip(sources, targets))
    ]
    for load in loads:
        load.start()

    barrier = pltpu.get_barrier_semaphore()

    def greet(step, carry):
        a, b = peer(step)
        pl.semaphore_signal(barrier, inc=1, device_id={"px": a, "pz": b})
        return carry

    pl.semaphore_signal(barrier, inc=1, device_id={"grp": 1 - grp})
    lax.fori_loop(1, SLABS, greet, 0)

    wave, shift = mode_turns(grp)
    for load in loads[:7]:
        load.wait()
    selection = block_fold(block_line[...])

    def deposit(turn, carry):
        first = pl.multiple_of(turn * 8, 8)
        here = pl.ds(first, 8)
        cells = cell[here, :]
        amount = volume[here, :]
        scale = amount * rate[here, :]
        angle = place[here, :] * TURN
        drags = [scale * (seen[c, here, :] - motion[c, here, :]) for c in range(3)]
        drags[1] = drags[1] - gravity * amount
        for i in range(8):
            phase = cosine_turns(
                wave * jnp.broadcast_to(angle[i : i + 1, :], (16, PT)) + shift
            )
            phases[first + i] = phase
            below = jnp.broadcast_to(cells[i : i + 1, :], (16, PT)) < 128
            lower, upper = [], []
            for c in range(3):
                payload = phase * jnp.broadcast_to(drags[c][i : i + 1, :], (16, PT))
                lower.append(jnp.where(below, payload, 0.0).astype(bf16))
                upper.append(jnp.where(below, 0.0, payload).astype(bf16))
            share = dot_t(
                jnp.concatenate(lower + upper, axis=0), one_hot_cells(cells[i : i + 1, :])
            )
            target = pl.ds(pl.multiple_of((first + i) * WIDTH, WIDTH), WIDTH)
            for h in range(2):
                shares[h, target, :] = share[WIDTH * h : WIDTH * h + WIDTH, :]
        return carry

    lax.fori_loop(0, TILES // 8, deposit, 0)

    def fold(c):
        for m in range(MODES):
            high, low = [], []
            for z in range(2):
                halves = [
                    shares[h, pl.ds(c * 16 + z * 8 + m, TILES, stride=WIDTH), :]
                    for h in range(2)
                ]
                value = jnp.concatenate(halves, axis=1)
                top = value.astype(bf16)
                high.append(top)
                low.append((value - top.astype(f32)).astype(bf16))
            sums = dot(selection, jnp.concatenate(high + low, axis=0))
            for q in range(4):
                for s in range(2):
                    first = q * 32 + s * 16
                    folded[q, m * 16 : m * 16 + 16, 256 * s : 256 * s + 256] = sums[
                        first : first + 16, :
                    ].astype(bf16)

    def forward(c):
        classes = []
        for q in range(4):
            even = dot(folded[q], tables[q, 0]).reshape(MODES, 2, ROWS, KEPT)
            odd = dot(folded[q], tables[q, 1]).reshape(MODES, 2, ROWS, KEPT)
            re = even[:, 0] + odd[:, 1]
            im = even[:, 1] - odd[:, 0]
            classes.append(
                jnp.concatenate([re, im], axis=1).reshape(MODES * 16, KEPT)
            )
        for h in range(2):
            chunks = swap_lanes([item[:, 128 * h : 128 * h + 128] for item in classes])
            for i in range(4):
                first = (4 * h + i) * 128
                forward_send[c, :, :, first : first + 128] = (
                    chunks[i].astype(bf16).reshape(MODES, 16, 128)
                )

    def forward_start(c):
        def send(step, carry):
            a, b = peer(step)
            pltpu.make_async_remote_copy(
                forward_send.at[c, b, :, pl.ds(pl.multiple_of(a * 128, 128), 128)],
                forward_recv.at[c, me],
                send_sem.at[c],
                recv_sem.at[c],
                device_id={"px": a, "pz": b},
            ).start()
            return carry

        pltpu.make_async_copy(
            forward_send.at[c, pz, :, pl.ds(pl.multiple_of(px * 128, 128), 128)],
            forward_recv.at[c, me],
            own_sem.at[c],
        ).start()
        lax.fori_loop(1, SLABS, send, 0)

    def back_start(c):
        def send(step, carry):
            a, b = peer(step)
            pltpu.make_async_remote_copy(
                back_send.at[c, a * N_PZ + b],
                back_recv.at[c, pz, :, pl.ds(pl.multiple_of(px * 128, 128), 128)],
                send_sem.at[3 + c],
                recv_sem.at[3 + c],
                device_id={"px": a, "pz": b},
            ).start()
            return carry

        pltpu.make_async_copy(
            back_send.at[c, me],
            back_recv.at[c, pz, :, pl.ds(pl.multiple_of(px * 128, 128), 128)],
            own_sem.at[3 + c],
        ).start()
        lax.fori_loop(1, SLABS, send, 0)

    def exchange_wait(index):
        blocks_in = forward_recv.at[0, pl.ds(0, SLABS - 1)]
        pltpu.make_async_remote_copy(
            blocks_in,
            blocks_in,
            send_sem.at[index],
            recv_sem.at[index],
            device_id={"px": px, "pz": pz},
        ).wait_recv()
        own = forward_recv.at[0, 0]
        pltpu.make_async_copy(own, own, own_sem.at[index]).wait()

    def sent_wait(index):
        blocks_out = forward_recv.at[0, pl.ds(0, SLABS - 1)]
        pltpu.make_async_remote_copy(
            blocks_out,
            blocks_out,
            send_sem.at[index],
            recv_sem.at[index],
            device_id={"px": px, "pz": pz},
        ).wait_send()

    fold(0)
    for load in loads[7:]:
        load.wait()
    forward(0)
    pl.semaphore_wait(barrier, SLABS)
    forward_start(0)
    for c in range(1, 3):
        fold(c)
        forward(c)
        forward_start(c)

    for matrix, split in ((basis, split_basis), (inverse, split_inverse)):
        high = matrix[...].astype(bf16)
        split[0] = high
        split[1] = (matrix[...] - high.astype(f32)).astype(bf16)
    lane = lax.broadcasted_iota(jnp.int32, (1, 128), 1)
    stream = px * 128 + 4 * (lane % 32) + lane // 32 - KX // 2
    stream = stream.astype(f32) * 0.5
    span = (grp * MODES + pz + 1).astype(f32)
    square = stream * stream + span * span
    column = jnp.transpose(jnp.broadcast_to(eigenvalues[...], (128, NY)))
    damping[...] = 1.0 / (1.0 + viscosity * (column + square))
    for c in range(3):
        for r in range(2):
            state = fluid[pl.ds(c * 2 + r, NY, stride=6), :]
            high = state.astype(bf16)
            low = (state - high.astype(f32)).astype(bf16)
            ordered[c, :, 128 * r : 128 * r + 128] = dot(
                jnp.concatenate([high, low], axis=1), order[...]
            )

    def apply(split, value):
        high = value.astype(bf16)
        low = (value - high.astype(f32)).astype(bf16)
        return dot(split[0], high) + (dot(split[0], low) + dot(split[1], high))

    for c in range(3):
        exchange_wait(c)
        forcing = forward_recv[c].astype(f32)
        force = jnp.concatenate(
            [forcing[:, 8 * r : 8 * r + 8, :].reshape(NY, 128) for r in range(2)], axis=1
        )
        modal = apply(split_inverse, ordered[c] + time_step * force)
        damp = damping[...]
        solved = apply(split_basis, modal * jnp.concatenate([damp, damp], axis=1))
        back_send[c] = jnp.concatenate(
            [solved[:, 128 * r : 128 * r + 128].reshape(SLABS, ROWS, 128) for r in range(2)],
            axis=1,
        ).astype(bf16)
        back_start(c)

    def backward(c):
        halves = []
        for h in range(2):
            parts = [
                back_recv[c, :, :, (4 * h + i) * 128 : (4 * h + i) * 128 + 128].reshape(
                    MODES * 16, 128
                )
                for i in range(4)
            ]
            halves.append(swap_lanes(parts))
        re, im = [], []
        for q in range(4):
            rows = jnp.concatenate([halves[0][q], halves[1][q]], axis=1)
            even = dot(rows, tables_back[q, 0]).reshape(MODES, 2, ROWS, FOLD)
            odd = dot(rows, tables_back[q, 1]).reshape(MODES, 2, ROWS, FOLD)
            re.append(even[:, 0] - odd[:, 1])
            im.append(odd[:, 0] + even[:, 1])
        sums = (re[0] + re[2], im[0] + im[2])
        lefts = (re[0] - re[2], im[0] - im[2])
        others = (re[1] + re[3], im[1] + im[3])
        rights = (im[3] - im[1], re[1] - re[3])
        results = (
            (sums[0] + others[0], sums[1] + others[1]),
            (lefts[0] + rights[0], lefts[1] + rights[1]),
            (sums[0] - others[0], sums[1] - others[1]),
            (lefts[0] - rights[0], lefts[1] - rights[1]),
        )
        for j in range(4):
            for r in range(2):
                for m in range(MODES):
                    for t in range(4):
                        planes[
                            pl.ds(m * 33 + (4 * j + t) * 2 + r, ROWS, stride=265), :
                        ] = results[j][r][m, :, 128 * t : 128 * t + 128]

        for y in range(ROWS):
            for s in range(STRIPS):
                for h in range(2):
                    pair = [
                        planes[pl.ds(y * 265 + (2 * s + h) * 2 + r, MODES, stride=33), :]
                        for r in range(2)
                    ]
                    blocks[c, y * STRIPS + s, :, 128 * h : 128 * h + 128] = jnp.concatenate(
                        pair, axis=0
                    ).astype(bf16)

    def write_planes(c):
        for y in range(ROWS):
            for m in range(MODES):
                planes_out[y, c, m * 32 : m * 32 + 32] = planes[
                    pl.ds(y * 265 + m * 33, 32), :
                ].astype(bf16)

    def part_copy(group, turn):
        here = (pl.ds(group[0], len(group)), pl.ds(pl.multiple_of(turn * 16, 16), 16))
        return pltpu.make_async_remote_copy(
            part_send.at[here],
            part_recv.at[here],
            part_send_sem.at[group[0], turn],
            part_recv_sem.at[group[0], turn],
            device_id={"grp": 1 - grp},
        )

    def sample(group):
        def sixteen_tiles(turn, carry):
            for half in range(2):
                first = pl.multiple_of(turn * 16 + 8 * half, 8)
                here = pl.ds(first, 8)
                cells = cell[here, :]
                lines = [[] for c in group]
                width = 16 * len(group)
                for i in range(8):
                    own_block = block[first + i]
                    rows = [blocks[c, own_block] for c in group]
                    rows = jnp.concatenate(
                        [item[:, :128] for item in rows] + [item[:, 128:] for item in rows], axis=0
                    )
                    both = dot(rows, one_hot_cells(cells[i : i + 1, :]))
                    below = jnp.broadcast_to(cells[i : i + 1, :], (width, PT)) < 128
                    picked = jnp.where(below, both[:width], both[width:])
                    phase = phases[first + i]
                    for n in range(len(group)):
                        lines[n].append(
                            jnp.sum(
                                picked[16 * n : 16 * n + 16, :] * phase, axis=0, keepdims=True
                            )
                        )
                for n, c in enumerate(group):
                    part[c, here, :] = jnp.concatenate(lines[n], axis=0)
            here = pl.ds(pl.multiple_of(turn * 16, 16), 16)
            for c in group:
                part_send[c, here, :] = part[c, here, :].astype(bf16)
            part_copy(group, turn).start()
            return carry

        lax.fori_loop(0, TILES // 16, sixteen_tiles, 0)

    def update(group):
        def sixteen_tiles(turn, carry):
            part_copy(group, turn).wait()
            here = pl.ds(pl.multiple_of(turn * 16, 16), 16)
            for c in group:
                fluid_at = part_send[c, here, :].astype(f32) + part_recv[c, here, :].astype(f32)
                old = motion[c, here, :]
                new = old + time_step * rate[here, :] * (fluid_at - old)
                updated[c, here, :] = new - time_step * gravity if c == 1 else new
            return carry

        lax.fori_loop(0, TILES // 16, sixteen_tiles, 0)

    for group in PASSES:
        for c in group:
            exchange_wait(3 + c)
            backward(c)
            if c < 2:
                write_planes(c)
        sample(group)
    write_planes(2)
    for group in PASSES:
        update(group)
    for index in range(6):
        sent_wait(index)


def deliver_kernel(planes, updated, planes_out, updated_out, sem):
    stores = [
        pltpu.make_async_copy(
            planes.at[pl.ds(2 * i, 2)], planes_out.at[pl.ds(2 * i, 2)], sem.at[i]
        )
        for i in range(4)
    ]
    stores.append(pltpu.make_async_copy(updated, updated_out, sem.at[4]))
    for store in stores:
        store.start()
    for store in stores:
        store.wait()


def on_device(
    cell_index,
    block_index,
    volume,
    response_rate,
    spanwise_position,
    particle_velocity,
    seen_velocity,
    fluid_velocity,
    eigen_basis,
    eigen_inverse,
    eigenvalues,
):
    tables = jnp.asarray(wave_tables())
    tables_back = jnp.asarray(np.swapaxes(wave_tables(), 2, 3).copy())
    order = jnp.asarray(lane_order())
    particles = ((TILES, PT), f32)
    vectors = ((3, TILES, PT), f32)
    scratch = (
        ((1, TILES), jnp.int32),
        ((1, NY), f32),
        (tables_back.shape, bf16),
        ((TILES, PT), jnp.int32),
        particles,
        particles,
        particles,
        vectors,
        vectors,
        (tables.shape, bf16),
        (order.shape, bf16),
        ((NY * 6, 128), f32),
        ((NY, NY), f32),
        ((NY, NY), f32),
        ((2, TILES * WIDTH, 128), f32),
        ((4, MODES * 16, FOLD), bf16),
        ((TILES, 16, PT), f32),
        ((2, NY, NY), bf16),
        ((2, NY, NY), bf16),
        ((NY, 128), f32),
        ((3, NY, 256), f32),
        ((3, MODES, 16, KX), bf16),
        ((3, SLABS, 16, 128), bf16),
        ((3, SLABS, 16, 128), bf16),
        ((3, MODES, 16, KX), bf16),
        ((2120, 128), f32),
        ((3, BLOCKS, 16, CB), bf16),
        vectors,
        ((3, TILES, PT), bf16),
        ((3, TILES, PT), bf16),
    )
    planes, updated = pl.pallas_call(
        flow_kernel,
        out_shape=(
            jax.ShapeDtypeStruct((ROWS, 3, MODES * 32, 128), bf16),
            jax.ShapeDtypeStruct((3, TILES, PT), f32),
        ),
        in_specs=[HBM] * 15,
        out_specs=(VMEM, VMEM),
        scratch_shapes=[pltpu.SMEM((TILES,), jnp.int32)]
        + [pltpu.VMEM(*item) for item in scratch]
        + [
            pltpu.SemaphoreType.DMA((15,)),
            pltpu.SemaphoreType.DMA((6,)),
            pltpu.SemaphoreType.DMA((6,)),
            pltpu.SemaphoreType.DMA((6,)),
            pltpu.SemaphoreType.DMA((3, TILES // 16)),
            pltpu.SemaphoreType.DMA((3, TILES // 16)),
        ],
        compiler_params=pltpu.CompilerParams(
            collective_id=0, has_side_effects=True, vmem_limit_bytes=36 * 2**20
        ),
        name="flow",
    )(*(
        pltpu.with_memory_space_constraint(item, pltpu.HBM)
        for item in (
        block_index,
        block_index.reshape(1, TILES),
        eigenvalues.reshape(1, NY),
        tables_back,
        cell_index,
        spanwise_position,
        volume,
        response_rate,
        particle_velocity,
        seen_velocity,
        tables,
        order,
        fluid_velocity.reshape(NY * 6, 128),
        eigen_basis,
        eigen_inverse,
            )
    ))
    planes, updated = pl.pallas_call(
        deliver_kernel,
        out_shape=(
            jax.ShapeDtypeStruct(planes.shape, bf16),
            jax.ShapeDtypeStruct((3, TILES, PT), f32),
        ),
        in_specs=[VMEM, VMEM],
        out_specs=(HBM, HBM),
        scratch_shapes=[pltpu.SemaphoreType.DMA((5,))],
        compiler_params=pltpu.CompilerParams(vmem_limit_bytes=8 * 2**20),
        name="deliver",
    )(planes, updated)
    planes = planes.reshape(ROWS, 3, MODES, 16, 2, 128)
    planes = jnp.transpose(planes, (0, 1, 2, 4, 3, 5)).reshape(ROWS, 3, MODES, 2, NX)
    return planes, updated


def solution(mesh):
    in_specs = (
        P(("px", "pz"), None),
        P(("px", "pz")),
        P(("px", "pz"), None),
        P(("px", "pz"), None),
        P(("px", "pz"), None),
        P(None, ("px", "pz"), None),
        P(None, ("px", "pz"), None),
        P(None, None, ("grp", "pz"), None, "px"),
        P(),
        P(),
        P(),
    )
    out_specs = (P(("px", "pz"), None, "grp", None, None), P(None, ("px", "pz"), None))
    return jax.shard_map(
        on_device, mesh=mesh, in_specs=in_specs, out_specs=out_specs, check_vma=False
    )
```

```python
import math

import jax
import jax.numpy as jnp
import ml_dtypes
import numpy as np
from jax import lax
from jax.experimental import pallas as pl
from jax.experimental.pallas import tpu as pltpu
from jax.sharding import PartitionSpec as P

NX = 2048
KX = 1024
NY = 512
CB = 256
PT = 512
TILES = 64
MODES = 8
ROWS = 8
STRIPS = 8
WIDTH = 3 * 2 * MODES
BLOCKS = ROWS * STRIPS
FOLD = NX // 4
KEPT = KX // 4
PASSES = ((0, 1), (2,))
N_PX = 8
N_PZ = 8
SLABS = N_PX * N_PZ
TURN = 1.0 / (2.0 * math.pi)
COSINE = (
    1.0,
    -19.73920440673828,
    64.93911743164062,
    -85.45011138916016,
    60.16743087768555,
    -25.96688461303711,
    6.527706146240234,
)

time_step = 0.5
gravity = 0.8
viscosity = 0.0001

f32 = jnp.float32
bf16 = jnp.bfloat16
VMEM = pl.BlockSpec(memory_space=pltpu.VMEM)
HBM = pl.BlockSpec(memory_space=pltpu.HBM)


def wave_tables():
    x = np.arange(FOLD, dtype=np.int64)[None, :, None]
    k = (
        4 * np.arange(KEPT, dtype=np.int64)[None, None, :]
        + np.arange(4, dtype=np.int64)[:, None, None]
        - KX // 2
    )
    angle = np.mod(k * x, NX) * (2.0 * math.pi / NX)
    table = np.stack([np.cos(angle), np.sin(angle)], axis=1) / math.sqrt(NX)
    return table.astype(np.float32).astype(ml_dtypes.bfloat16)


def lane_order():
    perm = np.zeros((128, 128), np.float32)
    lanes = np.arange(128)
    perm[4 * (lanes % 32) + lanes // 32, lanes] = 1.0
    return np.concatenate([perm, perm], axis=0).astype(ml_dtypes.bfloat16)


def cosine_turns(turns):
    part = turns - jnp.round(turns)
    square = part * part
    value = jnp.full_like(square, COSINE[-1])
    for term in COSINE[-2::-1]:
        value = value * square + term
    return value


def one_hot_cells(cell_row):
    cells = jnp.broadcast_to((cell_row & 127).astype(f32), (16, PT)).astype(bf16)
    lines = lax.broadcasted_iota(jnp.int32, (16, PT), 0).astype(f32).astype(bf16)
    one, zero = jnp.ones((16, PT), bf16), jnp.zeros((16, PT), bf16)
    return jnp.concatenate(
        [jnp.where(cells == lines + jnp.asarray(16 * i, bf16), one, zero) for i in range(8)],
        axis=0,
    )


def mode_turns(group):
    line = lax.broadcasted_iota(jnp.int32, (16, PT), 0)
    wave = (group * MODES + line % 8 + 1).astype(f32)
    shift = (line // 8).astype(f32) * 0.25
    return wave, shift


def swap_lanes(parts):
    return [
        jnp.concatenate([part[:, 32 * i : 32 * i + 32] for part in parts], axis=1)
        for i in range(4)
    ]


def dot(a, b):
    return lax.dot_general(a, b, (((1,), (0,)), ((), ())), preferred_element_type=f32)


def dot_t(a, b):
    return lax.dot_general(a, b, (((1,), (1,)), ((), ())), preferred_element_type=f32)


def block_fold(blocks_line):
    rows = lax.broadcasted_iota(jnp.int32, (128, 256), 0)
    lanes = lax.broadcasted_iota(jnp.int32, (128, 256), 1)
    q, s, r, y = rows // 32, (rows // 16) % 2, (rows // 8) % 2, rows % 8
    z = (lanes // TILES) % 2
    tile_block = jnp.broadcast_to(
        jnp.concatenate([blocks_line] * 4, axis=1), (128, 256)
    )
    strip = tile_block & 7
    turn = (q * (strip >> 1) + r - z + 4) & 3
    value = jnp.where(turn == 0, 1.0, jnp.where(turn == 2, -1.0, 0.0))
    here = ((tile_block >> 3) == y) & ((strip & 1) == s)
    return jnp.where(here, value, 0.0).astype(bf16)


def flow_kernel(
    block_any,
    block_line_any,
    eigenvalues_any,
    tables_back_any,
    cell_any,
    place_any,
    volume_any,
    rate_any,
    motion_any,
    seen_any,
    tables_any,
    order_any,
    fluid_any,
    basis_any,
    inverse_any,
    planes_out,
    updated,
    block,
    block_line,
    eigenvalues,
    tables_back,
    cell,
    place,
    volume,
    rate,
    motion,
    seen,
    tables,
    order,
    fluid,
    basis,
    inverse,
    shares,
    folded,
    phases,
    split_basis,
    split_inverse,
    damping,
    ordered,
    forward_send,
    forward_recv,
    back_send,
    back_recv,
    planes,
    blocks,
    part,
    part_send,
    part_recv,
    load_sem,
    own_sem,
    send_sem,
    recv_sem,
    part_send_sem,
    part_recv_sem,
):
    grp = lax.axis_index("grp")
    px = lax.axis_index("px")
    pz = lax.axis_index("pz")
    me = px * N_PZ + pz

    def peer(step):
        return lax.rem(px + step // N_PZ, N_PX), lax.rem(pz + lax.rem(step, N_PZ), N_PZ)

    sources = (cell_any, place_any, volume_any, rate_any, motion_any, seen_any)
    sources += (block_line_any, block_any, eigenvalues_any, tables_back_any, tables_any, order_any, fluid_any, basis_any, inverse_any)
    targets = (cell, place, volume, rate, motion, seen)
    targets += (block_line, block, eigenvalues, tables_back, tables, order, fluid, basis, inverse)
    loads = [
        pltpu.make_async_copy(source, target, load_sem.at[i])
        for i, (source, target) in enumerate(zip(sources, targets))
    ]
    for load in loads[:7]:
        load.start()

    barrier = pltpu.get_barrier_semaphore()

    def greet(step, carry):
        a, b = peer(step)
        pl.semaphore_signal(barrier, inc=1, device_id={"px": a, "pz": b})
        return carry

    pl.semaphore_signal(barrier, inc=1, device_id={"grp": 1 - grp})
    lax.fori_loop(1, SLABS, greet, 0)

    wave, shift = mode_turns(grp)
    for load in loads[:7]:
        load.wait()
    for load in loads[7:]:
        load.start()
    selection = block_fold(block_line[...])

    def deposit(turn, carry):
        first = pl.multiple_of(turn * 8, 8)
        here = pl.ds(first, 8)
        cells = cell[here, :]
        amount = volume[here, :]
        scale = amount * rate[here, :]
        angle = place[here, :] * TURN
        drags = [scale * (seen[c, here, :] - motion[c, here, :]) for c in range(3)]
        drags[1] = drags[1] - gravity * amount
        for i in range(8):
            phase = cosine_turns(
                wave * jnp.broadcast_to(angle[i : i + 1, :], (16, PT)) + shift
            )
            phases[first + i] = phase
            below = jnp.broadcast_to(cells[i : i + 1, :], (16, PT)) < 128
            lower, upper = [], []
            for c in range(3):
                payload = phase * jnp.broadcast_to(drags[c][i : i + 1, :], (16, PT))
                lower.append(jnp.where(below, payload, 0.0).astype(bf16))
                upper.append(jnp.where(below, 0.0, payload).astype(bf16))
            share = dot_t(
                jnp.concatenate(lower + upper, axis=0), one_hot_cells(cells[i : i + 1, :])
            )
            target = pl.ds(pl.multiple_of((first + i) * WIDTH, WIDTH), WIDTH)
            for h in range(2):
                shares[h, target, :] = share[WIDTH * h : WIDTH * h + WIDTH, :]
        return carry

    lax.fori_loop(0, TILES // 8, deposit, 0)

    def fold(c):
        for m in range(MODES):
            high, low = [], []
            for z in range(2):
                halves = [
                    shares[h, pl.ds(c * 16 + z * 8 + m, TILES, stride=WIDTH), :]
                    for h in range(2)
                ]
                value = jnp.concatenate(halves, axis=1)
                top = value.astype(bf16)
                high.append(top)
                low.append((value - top.astype(f32)).astype(bf16))
            sums = dot(selection, jnp.concatenate(high + low, axis=0))
            for q in range(4):
                for s in range(2):
                    first = q * 32 + s * 16
                    folded[q, m * 16 : m * 16 + 16, 256 * s : 256 * s + 256] = sums[
                        first : first + 16, :
                    ].astype(bf16)

    def forward(c):
        classes = []
        for q in range(4):
            even = dot(folded[q], tables[q, 0]).reshape(MODES, 2, ROWS, KEPT)
            odd = dot(folded[q], tables[q, 1]).reshape(MODES, 2, ROWS, KEPT)
            re = even[:, 0] + odd[:, 1]
            im = even[:, 1] - odd[:, 0]
            classes.append(
                jnp.concatenate([re, im], axis=1).reshape(MODES * 16, KEPT)
            )
        for h in range(2):
            chunks = swap_lanes([item[:, 128 * h : 128 * h + 128] for item in classes])
            for i in range(4):
                first = (4 * h + i) * 128
                forward_send[c, :, :, first : first + 128] = (
                    chunks[i].astype(bf16).reshape(MODES, 16, 128)
                )

    def forward_start(c):
        def send(step, carry):
            a, b = peer(step)
            pltpu.make_async_remote_copy(
                forward_send.at[c, b, :, pl.ds(pl.multiple_of(a * 128, 128), 128)],
                forward_recv.at[c, me],
                send_sem.at[c],
                recv_sem.at[c],
                device_id={"px": a, "pz": b},
            ).start()
            return carry

        pltpu.make_async_copy(
            forward_send.at[c, pz, :, pl.ds(pl.multiple_of(px * 128, 128), 128)],
            forward_recv.at[c, me],
            own_sem.at[c],
        ).start()
        lax.fori_loop(1, SLABS, send, 0)

    def back_start(c):
        def send(step, carry):
            a, b = peer(step)
            pltpu.make_async_remote_copy(
                back_send.at[c, a * N_PZ + b],
                back_recv.at[c, pz, :, pl.ds(pl.multiple_of(px * 128, 128), 128)],
                send_sem.at[3 + c],
                recv_sem.at[3 + c],
                device_id={"px": a, "pz": b},
            ).start()
            return carry

        pltpu.make_async_copy(
            back_send.at[c, me],
            back_recv.at[c, pz, :, pl.ds(pl.multiple_of(px * 128, 128), 128)],
            own_sem.at[3 + c],
        ).start()
        lax.fori_loop(1, SLABS, send, 0)

    def exchange_wait(index):
        blocks_in = forward_recv.at[0, pl.ds(0, SLABS - 1)]
        pltpu.make_async_remote_copy(
            blocks_in,
            blocks_in,
            send_sem.at[index],
            recv_sem.at[index],
            device_id={"px": px, "pz": pz},
        ).wait_recv()
        own = forward_recv.at[0, 0]
        pltpu.make_async_copy(own, own, own_sem.at[index]).wait()

    def sent_wait(index):
        blocks_out = forward_recv.at[0, pl.ds(0, SLABS - 1)]
        pltpu.make_async_remote_copy(
            blocks_out,
            blocks_out,
            send_sem.at[index],
            recv_sem.at[index],
            device_id={"px": px, "pz": pz},
        ).wait_send()

    fold(0)
    for load in loads[7:]:
        load.wait()
    forward(0)
    pl.semaphore_wait(barrier, SLABS)
    forward_start(0)
    for c in range(1, 3):
        fold(c)
        forward(c)
        forward_start(c)

    for matrix, split in ((basis, split_basis), (inverse, split_inverse)):
        high = matrix[...].astype(bf16)
        split[0] = high
        split[1] = (matrix[...] - high.astype(f32)).astype(bf16)
    lane = lax.broadcasted_iota(jnp.int32, (1, 128), 1)
    stream = px * 128 + 4 * (lane % 32) + lane // 32 - KX // 2
    stream = stream.astype(f32) * 0.5
    span = (grp * MODES + pz + 1).astype(f32)
    square = stream * stream + span * span
    column = jnp.transpose(jnp.broadcast_to(eigenvalues[...], (128, NY)))
    damping[...] = 1.0 / (1.0 + viscosity * (column + square))
    for c in range(3):
        for r in range(2):
            state = fluid[pl.ds(c * 2 + r, NY, stride=6), :]
            high = state.astype(bf16)
            low = (state - high.astype(f32)).astype(bf16)
            ordered[c, :, 128 * r : 128 * r + 128] = dot(
                jnp.concatenate([high, low], axis=1), order[...]
            )

    def apply(split, value):
        high = value.astype(bf16)
        low = (value - high.astype(f32)).astype(bf16)
        return dot(split[0], high) + (dot(split[0], low) + dot(split[1], high))

    for c in range(3):
        exchange_wait(c)
        forcing = forward_recv[c].astype(f32)
        force = jnp.concatenate(
            [forcing[:, 8 * r : 8 * r + 8, :].reshape(NY, 128) for r in range(2)], axis=1
        )
        modal = apply(split_inverse, ordered[c] + time_step * force)
        damp = damping[...]
        solved = apply(split_basis, modal * jnp.concatenate([damp, damp], axis=1))
        back_send[c] = jnp.concatenate(
            [solved[:, 128 * r : 128 * r + 128].reshape(SLABS, ROWS, 128) for r in range(2)],
            axis=1,
        ).astype(bf16)
        back_start(c)

    def backward(c):
        halves = []
        for h in range(2):
            parts = [
                back_recv[c, :, :, (4 * h + i) * 128 : (4 * h + i) * 128 + 128].reshape(
                    MODES * 16, 128
                )
                for i in range(4)
            ]
            halves.append(swap_lanes(parts))
        re, im = [], []
        for q in range(4):
            rows = jnp.concatenate([halves[0][q], halves[1][q]], axis=1)
            even = dot(rows, tables_back[q, 0]).reshape(MODES, 2, ROWS, FOLD)
            odd = dot(rows, tables_back[q, 1]).reshape(MODES, 2, ROWS, FOLD)
            re.append(even[:, 0] - odd[:, 1])
            im.append(odd[:, 0] + even[:, 1])
        sums = (re[0] + re[2], im[0] + im[2])
        lefts = (re[0] - re[2], im[0] - im[2])
        others = (re[1] + re[3], im[1] + im[3])
        rights = (im[3] - im[1], re[1] - re[3])
        results = (
            (sums[0] + others[0], sums[1] + others[1]),
            (lefts[0] + rights[0], lefts[1] + rights[1]),
            (sums[0] - others[0], sums[1] - others[1]),
            (lefts[0] - rights[0], lefts[1] - rights[1]),
        )
        for j in range(4):
            for r in range(2):
                for m in range(MODES):
                    for t in range(4):
                        planes[
                            pl.ds(m * 33 + (4 * j + t) * 2 + r, ROWS, stride=265), :
                        ] = results[j][r][m, :, 128 * t : 128 * t + 128]

        for y in range(ROWS):
            for s in range(STRIPS):
                for h in range(2):
                    pair = [
                        planes[pl.ds(y * 265 + (2 * s + h) * 2 + r, MODES, stride=33), :]
                        for r in range(2)
                    ]
                    blocks[c, y * STRIPS + s, :, 128 * h : 128 * h + 128] = jnp.concatenate(
                        pair, axis=0
                    ).astype(bf16)

    def write_planes(c):
        for y in range(ROWS):
            for m in range(MODES):
                planes_out[y, c, m * 32 : m * 32 + 32] = planes[
                    pl.ds(y * 265 + m * 33, 32), :
                ].astype(bf16)

    def part_copy(group, turn):
        here = (pl.ds(group[0], len(group)), pl.ds(pl.multiple_of(turn * 16, 16), 16))
        return pltpu.make_async_remote_copy(
            part_send.at[here],
            part_recv.at[here],
            part_send_sem.at[group[0], turn],
            part_recv_sem.at[group[0], turn],
            device_id={"grp": 1 - grp},
        )

    def sample(group):
        def sixteen_tiles(turn, carry):
            for half in range(2):
                first = pl.multiple_of(turn * 16 + 8 * half, 8)
                here = pl.ds(first, 8)
                cells = cell[here, :]
                lines = [[] for c in group]
                width = 16 * len(group)
                for i in range(8):
                    own_block = block[first + i]
                    rows = [blocks[c, own_block] for c in group]
                    rows = jnp.concatenate(
                        [item[:, :128] for item in rows] + [item[:, 128:] for item in rows], axis=0
                    )
                    both = dot(rows, one_hot_cells(cells[i : i + 1, :]))
                    below = jnp.broadcast_to(cells[i : i + 1, :], (width, PT)) < 128
                    picked = jnp.where(below, both[:width], both[width:])
                    phase = phases[first + i]
                    for n in range(len(group)):
                        lines[n].append(
                            jnp.sum(
                                picked[16 * n : 16 * n + 16, :] * phase, axis=0, keepdims=True
                            )
                        )
                for n, c in enumerate(group):
                    part[c, here, :] = jnp.concatenate(lines[n], axis=0)
            here = pl.ds(pl.multiple_of(turn * 16, 16), 16)
            for c in group:
                part_send[c, here, :] = part[c, here, :].astype(bf16)
            part_copy(group, turn).start()
            return carry

        lax.fori_loop(0, TILES // 16, sixteen_tiles, 0)

    def update(group):
        def sixteen_tiles(turn, carry):
            part_copy(group, turn).wait()
            here = pl.ds(pl.multiple_of(turn * 16, 16), 16)
            for c in group:
                fluid_at = part_send[c, here, :].astype(f32) + part_recv[c, here, :].astype(f32)
                old = motion[c, here, :]
                new = old + time_step * rate[here, :] * (fluid_at - old)
                updated[c, here, :] = new - time_step * gravity if c == 1 else new
            return carry

        lax.fori_loop(0, TILES // 16, sixteen_tiles, 0)

    for group in PASSES:
        for c in group:
            exchange_wait(3 + c)
            backward(c)
            if c < 2:
                write_planes(c)
        sample(group)
    write_planes(2)
    for group in PASSES:
        update(group)
    for index in range(6):
        sent_wait(index)


def deliver_kernel(planes, updated, planes_out, updated_out, sem):
    stores = [
        pltpu.make_async_copy(
            planes.at[pl.ds(2 * i, 2)], planes_out.at[pl.ds(2 * i, 2)], sem.at[i]
        )
        for i in range(4)
    ]
    stores.append(pltpu.make_async_copy(updated, updated_out, sem.at[4]))
    for store in stores:
        store.start()
    for store in stores:
        store.wait()


def on_device(
    cell_index,
    block_index,
    volume,
    response_rate,
    spanwise_position,
    particle_velocity,
    seen_velocity,
    fluid_velocity,
    eigen_basis,
    eigen_inverse,
    eigenvalues,
):
    tables = jnp.asarray(wave_tables())
    tables_back = jnp.asarray(np.swapaxes(wave_tables(), 2, 3).copy())
    order = jnp.asarray(lane_order())
    particles = ((TILES, PT), f32)
    vectors = ((3, TILES, PT), f32)
    scratch = (
        ((1, TILES), jnp.int32),
        ((1, NY), f32),
        (tables_back.shape, bf16),
        ((TILES, PT), jnp.int32),
        particles,
        particles,
        particles,
        vectors,
        vectors,
        (tables.shape, bf16),
        (order.shape, bf16),
        ((NY * 6, 128), f32),
        ((NY, NY), f32),
        ((NY, NY), f32),
        ((2, TILES * WIDTH, 128), f32),
        ((4, MODES * 16, FOLD), bf16),
        ((TILES, 16, PT), f32),
        ((2, NY, NY), bf16),
        ((2, NY, NY), bf16),
        ((NY, 128), f32),
        ((3, NY, 256), f32),
        ((3, MODES, 16, KX), bf16),
        ((3, SLABS, 16, 128), bf16),
        ((3, SLABS, 16, 128), bf16),
        ((3, MODES, 16, KX), bf16),
        ((2120, 128), f32),
        ((3, BLOCKS, 16, CB), bf16),
        vectors,
        ((3, TILES, PT), bf16),
        ((3, TILES, PT), bf16),
    )
    planes, updated = pl.pallas_call(
        flow_kernel,
        out_shape=(
            jax.ShapeDtypeStruct((ROWS, 3, MODES * 32, 128), bf16),
            jax.ShapeDtypeStruct((3, TILES, PT), f32),
        ),
        in_specs=[HBM] * 15,
        out_specs=(VMEM, VMEM),
        scratch_shapes=[pltpu.SMEM((TILES,), jnp.int32)]
        + [pltpu.VMEM(*item) for item in scratch]
        + [
            pltpu.SemaphoreType.DMA((15,)),
            pltpu.SemaphoreType.DMA((6,)),
            pltpu.SemaphoreType.DMA((6,)),
            pltpu.SemaphoreType.DMA((6,)),
            pltpu.SemaphoreType.DMA((3, TILES // 16)),
            pltpu.SemaphoreType.DMA((3, TILES // 16)),
        ],
        compiler_params=pltpu.CompilerParams(
            collective_id=0, has_side_effects=True, vmem_limit_bytes=36 * 2**20
        ),
        name="flow",
    )(*(
        pltpu.with_memory_space_constraint(item, pltpu.HBM)
        for item in (
        block_index,
        block_index.reshape(1, TILES),
        eigenvalues.reshape(1, NY),
        tables_back,
        cell_index,
        spanwise_position,
        volume,
        response_rate,
        particle_velocity,
        seen_velocity,
        tables,
        order,
        fluid_velocity.reshape(NY * 6, 128),
        eigen_basis,
        eigen_inverse,
            )
    ))
    planes, updated = pl.pallas_call(
        deliver_kernel,
        out_shape=(
            jax.ShapeDtypeStruct(planes.shape, bf16),
            jax.ShapeDtypeStruct((3, TILES, PT), f32),
        ),
        in_specs=[VMEM, VMEM],
        out_specs=(HBM, HBM),
        scratch_shapes=[pltpu.SemaphoreType.DMA((5,))],
        compiler_params=pltpu.CompilerParams(vmem_limit_bytes=8 * 2**20),
        name="deliver",
    )(planes, updated)
    planes = planes.reshape(ROWS, 3, MODES, 16, 2, 128)
    planes = jnp.transpose(planes, (0, 1, 2, 4, 3, 5)).reshape(ROWS, 3, MODES, 2, NX)
    return planes, updated


def solution(mesh):
    in_specs = (
        P(("px", "pz"), None),
        P(("px", "pz")),
        P(("px", "pz"), None),
        P(("px", "pz"), None),
        P(("px", "pz"), None),
        P(None, ("px", "pz"), None),
        P(None, ("px", "pz"), None),
        P(None, None, ("grp", "pz"), None, "px"),
        P(),
        P(),
        P(),
    )
    out_specs = (P(("px", "pz"), None, "grp", None, None), P(None, ("px", "pz"), None))
    return jax.shard_map(
        on_device, mesh=mesh, in_specs=in_specs, out_specs=out_specs, check_vma=False
    )
```
